128 devices in a mesh: seq: 32 (over y, z_hi, x), tp: 4 (over z_lo, core).
Axes of the slice: x: 4, y: 4, z: 4 (z_hi: 2, z_lo: 2; z = z_hi * 2 + z_lo), core: 2. Of those that a mesh axis runs over, the one named last changes fastest.
Arguments:
- query: bfloat16 [4096, 36864], P('seq', 'tp'), may hold values from -40 to 40
- latent: bfloat16 [4096, 576], P(('seq', 'tp')), may hold values from -5 to 5
- out_grad: bfloat16 [4096, 32768], P('seq', 'tp'), may hold values from -6 to 6
- positions: int32 [4096], P('seq'), may hold values from 0 to 4095, as said below
Outputs:
- query_grad: bfloat16 [4096, 36864], P('seq', 'tp')
- latent_grad: float32 [4096, 576], P(('seq', 'tp'))
The draws below stay inside these ranges and needn't reach their ends.
Inputs may be any that keep to these rules, and one draw needn't show every extreme that they name: positions is a permutation of 0 to 4095 made of aligned runs of 64 rows, each run holding 64 consecutive values in increasing order.
All inputs are finite; a program needn't handle non-finite values.
Results may differ from the reference program's by a relative error of at most 0.0047.
Values may be sent and summed in bfloat16 or wider, within the bound.
A program may use at most 192 MiB of HBM per device.

```python
import jax
import jax.numpy as jnp
from jax import lax

LAT = 512
ROPE = 64
HEADS = 64
KVW = 576
TOKENS = 4096
BLOCK = 64


def latent_base(key):
    return jnp.clip(jax.random.normal(key, (TOKENS, KVW), jnp.float32), -4.0, 4.0)


def draw_latent(key, part):
    base = latent_base(key)
    return base.astype(jnp.bfloat16)


def draw_query(key, part):
    key = jax.random.fold_in(key, 5)
    noise = jnp.clip(jax.random.normal(key, (TOKENS, HEADS, KVW), jnp.float32), -4.0, 4.0)
    return noise.reshape(TOKENS, HEADS * KVW).astype(jnp.bfloat16)


def draw_positions(key, part):
    key = jax.random.fold_in(key, 11)
    order = jax.random.permutation(key, TOKENS // BLOCK)
    places = order[:, None] * BLOCK + jnp.arange(BLOCK)[None, :]
    return places.reshape(TOKENS).astype(jnp.int32)


def steps_of(stream_key, extent, shards, smallest, high):
    loudness, own = 1.0, jax.random.fold_in(stream_key, 6)
    for axis_at, parts in shards:
        draws = jnp.exp(jax.random.uniform(jax.random.fold_in(own, axis_at), (parts,), jnp.float32, smallest / len(shards), high / len(shards)))
        loudness = loudness * jnp.repeat(draws, extent[axis_at] // parts).reshape([-1 if axis == axis_at else 1 for axis in range(len(extent))])
    return loudness


def normal_values(stream_key, extent, width, bound, split=(), kind=jnp.bfloat16):
    drawn = jax.random.normal(stream_key, extent, jnp.float32) * width
    if len(split) > 0:
        drawn = steps_of(stream_key, extent, split, -0.22, 0.18) * drawn
    return jnp.clip(drawn, min=-bound, max=bound).astype(kind)


def setup_inputs(seed: int = 0) -> dict:
    keys = jax.random.split(jax.random.key(seed), 5)
    return {
        "query": draw_query(jax.random.fold_in(keys[4], 71), 0),
        "latent": draw_latent(jax.random.fold_in(keys[4], 71), 0),
        "out_grad": normal_values(keys[2], (TOKENS, HEADS * LAT), 1.0, 6.0, ((0, 32), (1, 4))),
        "positions": draw_positions(jax.random.fold_in(keys[4], 71), 0),
    }


softmax_scale = 192.0 ** -0.5
masked_score = -1.0e30


def reference(query, latent, out_grad, positions):
    query_heads = jnp.transpose(query.reshape(TOKENS, HEADS, KVW), (1, 0, 2))
    grad_heads = jnp.transpose(out_grad.reshape(TOKENS, HEADS, LAT), (1, 0, 2))
    values = latent[:, :LAT]
    visible = positions[None, :] <= positions[:, None]

    def one_head(running, head_pair):
        query_head, grad_head = head_pair
        scores = jnp.dot(query_head, latent.T, preferred_element_type=jnp.float32) * softmax_scale
        scores = jnp.where(visible, scores, masked_score)
        row_top = jnp.max(scores, axis=1, keepdims=True)
        exponent = jnp.exp(scores - row_top)
        weights = exponent / jnp.sum(exponent, axis=1, keepdims=True)
        weights_half = weights.astype(jnp.bfloat16)
        grad_weights = jnp.dot(grad_head, values.T, preferred_element_type=jnp.float32)
        row_delta = jnp.sum(weights * grad_weights, axis=1, keepdims=True)
        grad_scores = (weights * (grad_weights - row_delta) * softmax_scale).astype(jnp.bfloat16)
        head_qgrad = jnp.dot(grad_scores, latent, preferred_element_type=jnp.float32).astype(jnp.bfloat16)
        key_grad = jnp.dot(grad_scores.T, query_head, preferred_element_type=jnp.float32)
        value_grad = jnp.dot(weights_half.T, grad_head, preferred_element_type=jnp.float32)
        running = running + key_grad + jnp.pad(value_grad, ((0, 0), (0, ROPE)))
        return running, head_qgrad

    running, head_grads = lax.scan(one_head, jnp.zeros((TOKENS, KVW), jnp.float32), (query_heads, grad_heads))
    query_grad = jnp.transpose(head_grads, (1, 0, 2)).reshape(TOKENS, HEADS * KVW)
    return query_grad, running
```

```python
import functools
import math

import jax, jax.numpy as jnp
from jax import lax
from jax.experimental import pallas as pl
from jax.experimental.pallas import tpu as pltpu
from jax.sharding import PartitionSpec as P

LAT=512; KVW=576; PAD=640
MESH = pl.DeviceIdType.MESH
PARTS = (((0, 1, 2), 0, 256), ((1, 2, 0), 256, 256), ((2, 0, 1), 512, 128))


def coords():
    seq, tp = lax.axis_index("seq"), lax.axis_index("tp")
    x = lax.rem(seq, 4)
    z = lax.rem(seq // 4, 2) * 2 + tp // 2
    y = seq // 8
    return [x, y, z], lax.rem(tp, 2)


def device(place, core):
    x, y, z = place
    return ((y * 2 + z // 2) * 4 + x, lax.rem(z, 2) * 2 + core)


def moved(place, axis, by):
    out = list(place)
    out[axis] = lax.rem(place[axis] + by, 4)
    return out


def greet(place, core):
    barrier = pltpu.get_barrier_semaphore()
    for axis in range(3):
        for by in (1, 3):
            pl.semaphore_signal(barrier, inc=1, device_id=device(moved(place, axis, by), core), device_id_type=MESH)
    pl.semaphore_signal(barrier, inc=1, device_id=device(place, 1 - core), device_id_type=MESH)
    pl.semaphore_wait(barrier, 7)


def gather_kernel(pos_ref, lat_ref, out_ref, own, sem, send, recv):
    place, core = coords()
    greet(place, core)
    run = pos_ref[lax.rem(place[2], 2) * 64] // 64
    own[:, :KVW] = lat_ref[...]
    own[:, KVW:] = jnp.full((32, PAD - KVW), run.astype(jnp.float32)).astype(jnp.bfloat16)
    put = pltpu.make_async_copy(own, out_ref.at[core, place[0], place[1], place[2]], sem)
    put.start()
    put.wait()
    count = [0]
    sent = []

    def copy(ref, dev):
        i = count[0]
        count[0] += 1
        c = pltpu.make_async_remote_copy(ref, ref, send.at[i], recv.at[i], device_id=dev, device_id_type=MESH)
        c.start()
        sent.append(c)
        return c

    def view(done, axis, value, rows, lane, width):
        at = [pl.ds(0, 4) if a in done else place[a] for a in range(3)]
        at[axis] = value
        return out_ref.at[core, at[0], at[1], at[2], pl.ds(*rows), pl.ds(lane, width)]

    both = (0, 32)
    sibling = device(place, 1 - core)
    twins = []
    twins.append(copy(out_ref.at[core, place[0], place[1], place[2]], sibling))
    for phase in range(3):
        first = []
        for order, lane, width in PARTS:
            axis, done = order[phase], order[:phase]
            mine = view(done, axis, place[axis], both, lane, width)
            r = copy(mine, device(moved(place, axis, 1), core))
            l = copy(mine, device(moved(place, axis, 3), core))
            first.append((r, l))
        second = []
        for (order, lane, width), (r, l) in zip(PARTS, first):
            axis, done = order[phase], order[:phase]
            right, left = lax.rem(place[axis] + 1, 4), lax.rem(place[axis] + 3, 4)
            r.wait_recv()
            a = copy(view(done, axis, left, (0, 16), lane, width), device(moved(place, axis, 1), core))
            l.wait_recv()
            b = copy(view(done, axis, right, (16, 16), lane, width), device(moved(place, axis, 3), core))
            twins.append(copy(view(done, axis, left, both, lane, width), sibling))
            twins.append(copy(view(done, axis, right, both, lane, width), sibling))
            second.append((a, b))
        for (order, lane, width), (a, b) in zip(PARTS, second):
            axis, done = order[phase], order[:phase]
            a.wait_recv()
            b.wait_recv()
            twins.append(copy(view(done, axis, lax.rem(place[axis] + 2, 4), both, lane, width), sibling))
    for t in twins:
        t.wait_recv()
    for s in sent:
        s.wait_send()


N_GATHER = 1 + 3 * 3 * 7


def gather(positions, latent):
    return pl.pallas_call(
        gather_kernel,
        out_shape=jax.ShapeDtypeStruct((2, 4, 4, 4, 32, PAD), jnp.bfloat16),
        in_specs=[pl.BlockSpec(memory_space=pltpu.SMEM), pl.BlockSpec(memory_space=pltpu.VMEM)],
        out_specs=pl.BlockSpec(memory_space=pl.ANY),
        scratch_shapes=[
            pltpu.VMEM((32, PAD), jnp.bfloat16),
            pltpu.SemaphoreType.DMA,
            pltpu.SemaphoreType.DMA((N_GATHER,)),
            pltpu.SemaphoreType.DMA((N_GATHER,)),
        ],
        compiler_params=pltpu.CompilerParams(collective_id=0, has_side_effects=True),
        cost_estimate=pl.CostEstimate(flops=0, bytes_accessed=10 * 2**20, transcendentals=0),
        name="gather_latent",
    )(positions, latent)


def dropped(axis, done):
    return axis - sum(1 for a in done if a < axis)


def at(ref, dim, value, rows=None):
    index = [slice(None)] * dim + [value]
    view = ref.at[tuple(index)]
    if rows is not None:
        lead = len(view.shape) - 2
        view = view.at[tuple([slice(None)] * lead + [pl.ds(*rows)])]
    return view


def scatter_kernel(wires, part_ref, out_ref, mine, theirs, keep, wire, relay, landed, sem, send, recv):
    place, core = coords()
    greet(place, core)
    count = [0]
    sent = []

    def copy(src, dst, dev):
        i = count[0]
        count[0] += 1
        c = pltpu.make_async_remote_copy(src, dst, send.at[i], recv.at[i], device_id=dev, device_id_type=MESH)
        c.start()
        sent.append(c)
        return c

    sibling = device(place, 1 - core)
    swaps, loads = [], []
    for n, (order, lane, width) in enumerate(PARTS):
        other = part_ref.at[:, :, :, pl.ds(32 * (1 - core), 32), pl.ds(lane, width)]
        swaps.append(copy(other, theirs[n], sibling))
        load = pltpu.make_async_copy(part_ref.at[:, :, :, pl.ds(32 * core, 32), pl.ds(lane, width)], mine[n], sem.at[n])
        load.start()
        loads.append(load)

    halves = ((0, 16), (16, 16))
    for phase in range(3):
        started = []
        for n, (order, lane, width) in enumerate(PARTS):
            axis, done = order[phase], order[:phase]
            dim = dropped(axis, done)
            k, w, rl, ld = keep[n][phase], wire[n][phase], relay[n][phase], landed[n][phase]
            me = place[axis]
            right, left, opp = (lax.rem(me + i, 4) for i in (1, 3, 2))
            rdev, ldev = device(moved(place, axis, 1), core), device(moved(place, axis, 3), core)
            if phase == 0:
                loads[n].wait()
                swaps[n].wait_recv()
                def fill(v):
                    at(k, dim, v)[...] = at(mine[n], dim, v)[...].astype(jnp.float32) + at(theirs[n], dim, v)[...].astype(jnp.float32)
            else:
                def fill(v):
                    pass
            fill(opp)
            at(w, dim, opp)[...] = at(k, dim, opp)[...].astype(w.dtype)
            c0 = copy(at(w, dim, opp, halves[0]), rl.at[0], rdev)
            c1 = copy(at(w, dim, opp, halves[1]), rl.at[1], ldev)
            fill(right)
            at(w, dim, right, halves[1])[...] = at(k, dim, right, halves[1])[...].astype(w.dtype)
            c2 = copy(at(w, dim, right, halves[1]), ld.at[0, 1], rdev)
            fill(left)
            at(w, dim, left, halves[0])[...] = at(k, dim, left, halves[0])[...].astype(w.dtype)
            c3 = copy(at(w, dim, left, halves[0]), ld.at[1, 0], ldev)
            fill(me)
            started.append((c0, c1, c2, c3))
        ended = []
        for n, (order, lane, width) in enumerate(PARTS):
            axis, done = order[phase], order[:phase]
            dim = dropped(axis, done)
            k, w, rl, ld = keep[n][phase], wire[n][phase], relay[n][phase], landed[n][phase]
            me = place[axis]
            right, left = lax.rem(me + 1, 4), lax.rem(me + 3, 4)
            rdev, ldev = device(moved(place, axis, 1), core), device(moved(place, axis, 3), core)
            c0, c1, c2, c3 = started[n]
            c0.wait_recv()
            at(w, dim, right, halves[0])[...] = (at(k, dim, right, halves[0])[...] + rl[0].astype(jnp.float32)).astype(w.dtype)
            c4 = copy(at(w, dim, right, halves[0]), ld.at[0, 0], rdev)
            c1.wait_recv()
            at(w, dim, left, halves[1])[...] = (at(k, dim, left, halves[1])[...] + rl[1].astype(jnp.float32)).astype(w.dtype)
            c5 = copy(at(w, dim, left, halves[1]), ld.at[1, 1], ldev)
            ended.append((c2, c3, c4, c5))
        for n, (order, lane, width) in enumerate(PARTS):
            axis, done = order[phase], order[:phase]
            dim = dropped(axis, done)
            k, ld = keep[n][phase], landed[n][phase]
            for c in ended[n]:
                c.wait_recv()
            for h in (0, 1):
                total = (at(k, dim, place[axis], halves[h])[...] + ld[0, h].astype(jnp.float32)) + ld[1, h].astype(jnp.float32)
                if phase < 2:
                    to = keep[n][phase + 1]
                    to.at[tuple([slice(None)] * (2 - phase) + [pl.ds(*halves[h])])][...] = total
                else:
                    real = min(width, KVW - lane)
                    out_ref[pl.ds(*halves[h]), pl.ds(lane, real)] = total[:, :real]
    for s in sent:
        s.wait_send()


N_SCATTER = 3 + 9 * 6


def scatter(part, wires=(jnp.bfloat16, jnp.float32, jnp.float32)):
    V = pltpu.VMEM
    mine = [V((4, 4, 4, 32, w), jnp.bfloat16) for _, _, w in PARTS]
    keep = [[V((4,) * (3 - p) + (32, w), jnp.float32) for p in range(3)] for _, _, w in PARTS]
    wire = [[V((4,) * (3 - p) + (32, w), wires[p]) for p in range(3)] for _, _, w in PARTS]
    relay = [[V((2,) + (4,) * (2 - p) + (16, w), wires[p]) for p in range(3)] for _, _, w in PARTS]
    landed = [[V((2, 2) + (4,) * (2 - p) + (16, w), wires[p]) for p in range(3)] for _, _, w in PARTS]
    return pl.pallas_call(
        functools.partial(scatter_kernel, wires),
        out_shape=jax.ShapeDtypeStruct((32, KVW), jnp.float32),
        in_specs=[pl.BlockSpec(memory_space=pl.ANY)],
        out_specs=pl.BlockSpec(memory_space=pltpu.VMEM),
        scratch_shapes=[
            mine, list(mine), keep, wire, relay, landed,
            pltpu.SemaphoreType.DMA((3,)),
            pltpu.SemaphoreType.DMA((N_SCATTER,)),
            pltpu.SemaphoreType.DMA((N_SCATTER,)),
        ],
        compiler_params=pltpu.CompilerParams(collective_id=1, has_side_effects=True, vmem_limit_bytes=40 * 2**20),
        cost_estimate=pl.CostEstimate(flops=0, bytes_accessed=10 * 2**20, transcendentals=0),
        name="scatter_latent_grad",
    )(part)


SCALE = 192.0 ** -0.5
TO_BASE_2 = SCALE * math.log2(math.e)
MASKED = -1e30
TOKENS = 4096
RUN = 64
RUNS = TOKENS // RUN
HEADS = 16
GROUP = 8
ROWS = GROUP * RUN
BIG, SMALL = 1024, 512


def attend_kernel(chip_run, own_run, q_ref, do_ref, kg_ref, qg_ref, part_ref,
                  chip_of, keys, keys_t, acc, exps, gws, tops, qs, qs_t, dos, dos_t, qg_t, q_in, do_in, qg_out,
                  key_sem, in_sem, out_sem):
    f32, bf16 = jnp.float32, jnp.bfloat16
    copy_q = pltpu.make_async_copy(q_ref, q_in, in_sem.at[0])
    copy_do = pltpu.make_async_copy(do_ref, do_in, in_sem.at[1])

    def place(chip, _):
        run = chip_run[chip]
        chip_of[run] = chip
        for c in range(2):
            pltpu.make_async_copy(kg_ref.at[c, chip], keys.at[pl.ds(run * RUN + c * 32, 32)], key_sem).start()
        return 0

    lax.fori_loop(0, RUNS, place, 0)
    copy_q.start()
    copy_do.start()
    acc[...] = jnp.zeros_like(acc)
    qs[:, LAT:] = jnp.zeros((ROWS, PAD - LAT), bf16)
    pltpu.make_async_copy(keys, keys, key_sem).wait()

    def turn(j, _):
        o = pl.multiple_of(j * 256, 256)
        keys_t[:, pl.ds(o, 256)] = keys[pl.ds(o, 256), :].T
        return 0

    lax.fori_loop(0, TOKENS // 256, turn, 0)
    copy_q.wait()
    copy_do.wait()

    def chunk(c, _):
        half, block = lax.rem(c, 2), c // 2
        run = own_run[block]
        row = pl.multiple_of(block * RUN, RUN)
        for h in range(0, GROUP, 2):
            v = q_in[pl.ds(row, RUN), pl.ds(pl.multiple_of(half * (GROUP * KVW) + h * KVW, 128), 2 * KVW)]
            qs[h * RUN:h * RUN + RUN, :KVW] = v[:, :KVW]
            qs[h * RUN + RUN:h * RUN + 2 * RUN, :KVW] = v[:, KVW:]
            d = do_in[pl.ds(row, RUN), pl.ds(pl.multiple_of(half * (GROUP * LAT) + h * LAT, 128), 2 * LAT)]
            dos[h * RUN:h * RUN + RUN, :] = d[:, :LAT]
            dos[h * RUN + RUN:h * RUN + 2 * RUN, :] = d[:, LAT:]
        qs_t[...] = qs[...].T
        dos_t[...] = dos[...].T
        small = run // (SMALL // RUN)
        bulk = small // 2

        def scan(t, size, masked, carry):
            m, l, d = carry
            o = pl.multiple_of(t * BIG, BIG)
            tile = keys[pl.ds(o, size), :]
            s = jnp.dot(tile, qs_t[...], preferred_element_type=f32)
            g = jnp.dot(tile[:, :LAT], dos_t[...], preferred_element_type=f32)
            if masked:
                key = lax.broadcasted_iota(jnp.int32, (size, ROWS), 0)
                tok = lax.broadcasted_iota(jnp.int32, (size, ROWS), 1) % RUN
                s = jnp.where(key - tok <= run * RUN - o, s, MASKED)
            s = s * TO_BASE_2
            top = jnp.maximum(m, jnp.max(s, axis=0, keepdims=True))
            e = jnp.exp2(s - top)
            exps[pl.ds(o, size), :] = e
            gws[pl.ds(o, size), :] = g
            tops[pl.ds(t * 8, 8), :] = jnp.broadcast_to(top, (8, ROWS))
            a = jnp.exp2(m - top)
            return top, l * a + jnp.sum(e, axis=0, keepdims=True), d * a + jnp.sum(e * g, axis=0, keepdims=True)

        start = (jnp.full((1, ROWS), MASKED, f32), jnp.zeros((1, ROWS), f32), jnp.zeros((1, ROWS), f32))
        carry = lax.fori_loop(0, bulk, lambda t, s: scan(t, BIG, False, s), start)
        m, l, d = lax.cond(lax.rem(small, 2) == 1, lambda: scan(bulk, BIG, True, carry), lambda: scan(bulk, SMALL, True, carry))
        share = 1.0 / l
        delta = d * share
        qg_t[...] = jnp.zeros_like(qg_t)

        def back(t, size):
            o = pl.multiple_of(t * BIG, BIG)
            span = pl.ds(o, size)
            w = exps[span, :] * (jnp.exp2(tops[pl.ds(t * 8, 8), :][:1] - m) * share)
            ds = (w * ((gws[span, :] - delta) * SCALE)).astype(bf16)
            acc[span, :LAT] += (jnp.dot(ds, qs[:, :LAT], preferred_element_type=f32)
                                + jnp.dot(w.astype(bf16), dos[...], preferred_element_type=f32))
            acc[span, LAT:] += jnp.dot(ds, qs[:, LAT:], preferred_element_type=f32)
            qg_t[...] += jnp.dot(keys_t[:KVW, span], ds, preferred_element_type=f32)

        def bulk_back(t, _):
            back(t, BIG)
            return 0

        lax.fori_loop(0, bulk, bulk_back, 0)
        pl.when(lax.rem(small, 2) == 1)(lambda: back(bulk, BIG))
        pl.when(lax.rem(small, 2) == 0)(lambda: back(bulk, SMALL))
        for h in range(0, GROUP, 2):
            a = qg_t[:, h * RUN:h * RUN + 2 * RUN].T.astype(bf16)
            qg_out[pl.ds(row, RUN), pl.ds(pl.multiple_of(half * (GROUP * KVW) + h * KVW, 128), 2 * KVW)] = jnp.concatenate([a[:RUN], a[RUN:]], axis=1)
        return 0

    lax.fori_loop(0, 4, chunk, 0)
    copy_out = pltpu.make_async_copy(qg_out, qg_ref, in_sem.at[0])
    copy_out.start()

    def leave(j, _):
        o = pl.multiple_of(j * 256, 256)
        keys[pl.ds(o, 256), :] = acc[pl.ds(o, 256), :].astype(bf16)
        for i in range(4):
            pltpu.make_async_copy(keys.at[pl.ds(o + i * RUN, RUN)], part_ref.at[chip_of[j * 4 + i]], out_sem).start()
        return 0

    lax.fori_loop(0, TOKENS // 256, leave, 0)
    pltpu.make_async_copy(keys, keys, out_sem).wait()
    copy_out.wait()


def attend(chip_run, own_run, query, out_grad, gathered):
    V, f32, bf16 = pltpu.VMEM, jnp.float32, jnp.bfloat16
    return pl.pallas_call(
        attend_kernel,
        out_shape=(jax.ShapeDtypeStruct((2 * RUN, HEADS * KVW), bf16), jax.ShapeDtypeStruct((RUNS, RUN, PAD), bf16)),
        in_specs=[pl.BlockSpec(memory_space=pltpu.SMEM)] * 2 + [pl.BlockSpec(memory_space=pl.ANY)] * 3,
        out_specs=(pl.BlockSpec(memory_space=pl.ANY),) * 2,
        scratch_shapes=[
            pltpu.SMEM((RUNS,), jnp.int32),
            V((TOKENS, PAD), bf16), V((PAD, TOKENS), bf16), V((TOKENS, PAD), f32),
            V((TOKENS, ROWS), f32), V((TOKENS, ROWS), f32), V((TOKENS // BIG * 8, ROWS), f32),
            V((ROWS, PAD), bf16), V((PAD, ROWS), bf16), V((ROWS, LAT), bf16), V((LAT, ROWS), bf16),
            V((KVW, ROWS), f32),
            V((2 * RUN, HEADS * KVW), bf16), V((2 * RUN, HEADS * LAT), bf16), V((2 * RUN, HEADS * KVW), bf16),
            pltpu.SemaphoreType.DMA, pltpu.SemaphoreType.DMA((2,)), pltpu.SemaphoreType.DMA,
        ],
        compiler_params=pltpu.CompilerParams(vmem_limit_bytes=60 * 2**20),
        cost_estimate=pl.CostEstimate(flops=46 * 10**9, bytes_accessed=2 * 10**7, transcendentals=10**7),
        name="attend",
    )(chip_run, own_run, query, out_grad, gathered)


def per_device(query, latent, out_grad, positions):
    gathered = gather(positions, latent)
    chip_run = gathered[0, :, :, :, 0, KVW].astype(jnp.int32).reshape(RUNS)
    own_run = positions[::RUN] // RUN
    query_grad, part = attend(chip_run, own_run, query, out_grad, gathered.reshape(2, RUNS, 32, PAD))
    return query_grad, scatter(part.reshape(4, 4, 4, RUN, PAD))


def solution(mesh):
    return jax.shard_map(
        per_device,
        mesh=mesh,
        in_specs=(P("seq", "tp"), P(("seq", "tp"), None), P("seq", "tp"), P("seq")),
        out_specs=(P("seq", "tp"), P(("seq", "tp"), None)),
        check_vma=False,
    )
```

```python
import math

import jax, jax.numpy as jnp
from jax import lax
from jax.experimental import pallas as pl
from jax.experimental.pallas import tpu as pltpu
from jax.sharding import PartitionSpec as P

LAT=512; KVW=576; PAD=640
SCALE = 192.0 ** -0.5
TO_BASE_2 = SCALE * math.log2(math.e)
MASKED = -1e30
TOKENS = 4096
RUN = 64
RUNS = TOKENS // RUN
HEADS = 16
GROUP = 8
ROWS = GROUP * RUN
BIG, SMALL = 1024, 512
CHUNKS = 2 * HEADS // GROUP
QUARTERS = TOKENS // BIG
SLICES = CHUNKS * QUARTERS
PLAN = (4, 4, 3, 2, 1, 1, 1)
MESH = pl.DeviceIdType.MESH
PARTS = (((0, 1, 2), 0, 256), ((1, 2, 0), 256, 256), ((2, 0, 1), 512, 128))


def coords():
    seq, tp = lax.axis_index("seq"), lax.axis_index("tp")
    x = lax.rem(seq, 4)
    z = lax.rem(seq // 4, 2) * 2 + tp // 2
    y = seq // 8
    return [x, y, z], lax.rem(tp, 2)


def device(place, core):
    x, y, z = place
    return ((y * 2 + z // 2) * 4 + x, lax.rem(z, 2) * 2 + core)


def moved(place, axis, by):
    out = list(place)
    out[axis] = lax.rem(place[axis] + by, 4)
    return out


def greet(place, core, opposite=False):
    barrier = pltpu.get_barrier_semaphore()
    steps = (1, 2, 3) if opposite else (1, 3)
    for axis in range(3):
        for by in steps:
            pl.semaphore_signal(barrier, inc=1, device_id=device(moved(place, axis, by), core), device_id_type=MESH)
    pl.semaphore_signal(barrier, inc=1, device_id=device(place, 1 - core), device_id_type=MESH)
    pl.semaphore_wait(barrier, 3 * len(steps) + 1)


def gather_kernel(pos_ref, lat_ref, out_ref, own, sem, send, recv):
    place, core = coords()
    run = pos_ref[lax.rem(place[2], 2) * 64] // 64
    own[:, :KVW] = lat_ref[...]
    own[:, KVW:] = jnp.full((32, PAD - KVW), run.astype(jnp.float32)).astype(jnp.bfloat16)
    put = pltpu.make_async_copy(own, out_ref.at[core, place[0], place[1], place[2]], sem)
    put.start()
    greet(place, core, True)
    put.wait()
    sent = []

    def copy(ref, dev):
        i = len(sent)
        c = pltpu.make_async_remote_copy(ref, ref, send.at[i], recv.at[i], device_id=dev, device_id_type=MESH)
        c.start()
        sent.append(c)
        return c

    def shards(order, lane, width, at1, at2, at3, rows=(0, 32)):
        at = [None] * 3
        for axis, v in zip(order, (at1, at2, at3)):
            at[axis] = pl.ds(0, 4) if v is None else lax.rem(place[axis] + v, 4)
        return out_ref.at[core, at[0], at[1], at[2], pl.ds(*rows), pl.ds(lane, width)]

    sibling = device(place, 1 - core)
    twins = []
    one, two, three = {}, {}, {}
    steps = (1, 3, 2)

    def spread(p, d1):
        order, lane, width = PARTS[p]
        for by in steps:
            two[p, d1, by] = copy(shards(order, lane, width, d1, 0, 0), device(moved(place, order[1], by), core))

    def shift(p, d2):
        order, lane, width = PARTS[p]
        for by in (1, 3):
            three[p, d2, by] = copy(shards(order, lane, width, None, d2, 0), device(moved(place, order[2], by), core))

    def forward(p, d2):
        order, lane, width = PARTS[p]
        three[p, d2, 1].wait_recv()
        three[p, d2, 4] = copy(shards(order, lane, width, None, d2, 3, (0, 16)), device(moved(place, order[2], 1), core))
        three[p, d2, 3].wait_recv()
        three[p, d2, 5] = copy(shards(order, lane, width, None, d2, 1, (16, 16)), device(moved(place, order[2], 3), core))

    def arrive(p, d2):
        for d1 in (0, 1, 3, 2):
            two[p, d1, {3: 1, 1: 3, 2: 2}[d2]].wait_recv()

    n = range(len(PARTS))
    for p in n:
        order, lane, width = PARTS[p]
        for by in steps:
            one[p, by] = copy(shards(order, lane, width, 0, 0, 0), device(moved(place, order[0], by), core))
    for p in n:
        spread(p, 0)
    for by in steps:
        for p in n:
            one[p, by].wait_recv()
            spread(p, {1: 3, 3: 1, 2: 2}[by])
    for p in n:
        shift(p, 0)
    for d2 in (3, 1, 2):
        for p in n:
            arrive(p, d2)
            shift(p, d2)
    for p in n:
        order, lane, width = PARTS[p]
        twins.append(copy(shards(order, lane, width, None, None, 0), sibling))
    for d2 in (0, 3, 1, 2):
        for p in n:
            forward(p, d2)
    for p in n:
        order, lane, width = PARTS[p]
        twins.append(copy(shards(order, lane, width, None, None, 3), sibling))
        twins.append(copy(shards(order, lane, width, None, None, 1), sibling))
    for d2 in (0, 3, 1, 2):
        for p in n:
            order, lane, width = PARTS[p]
            three[p, d2, 4].wait_recv()
            three[p, d2, 5].wait_recv()
            twins.append(copy(shards(order, lane, width, None, d2, 2), sibling))
    for t in twins:
        t.wait_recv()
    for s in sent:
        s.wait_send()


N_GATHER = 3 * (3 + 12 + 8 + 1 + 8 + 2 + 4)


def gather(positions, latent):
    return pl.pallas_call(
        gather_kernel,
        out_shape=jax.ShapeDtypeStruct((2, 4, 4, 4, 32, PAD), jnp.bfloat16),
        in_specs=[pl.BlockSpec(memory_space=pltpu.SMEM), pl.BlockSpec(memory_space=pltpu.VMEM)],
        out_specs=pl.BlockSpec(memory_space=pl.ANY),
        scratch_shapes=[
            pltpu.VMEM((32, PAD), jnp.bfloat16),
            pltpu.SemaphoreType.DMA,
            pltpu.SemaphoreType.DMA((N_GATHER,)),
            pltpu.SemaphoreType.DMA((N_GATHER,)),
        ],
        compiler_params=pltpu.CompilerParams(collective_id=0, has_side_effects=True),
        cost_estimate=pl.CostEstimate(flops=0, bytes_accessed=10 * 2**20, transcendentals=0),
        name="gather_latent",
    )(positions, latent)


def dropped(axis, done):
    return axis - sum(1 for a in done if a < axis)


def at(ref, dim, value, rows=None):
    index = [slice(None)] * dim + [value]
    view = ref.at[tuple(index)]
    if rows is not None:
        lead = len(view.shape) - 2
        view = view.at[tuple([slice(None)] * lead + [pl.ds(*rows)])]
    return view


def scatter_kernel(part_ref, ds_ref, kt_ref, out_ref, qg_ref, mine, theirs, keep, wire, relay, landed,
                   keys_t, ds_in, qg_t, qg_out, sem, kt_sem, ds_sem, qg_sem, send, recv):
    place, core = coords()
    load_kt = pltpu.make_async_copy(kt_ref, keys_t, kt_sem)
    load_kt.start()

    def load_ds(i):
        return pltpu.make_async_copy(ds_ref.at[i // QUARTERS, pl.ds(lax.rem(i, QUARTERS) * BIG, BIG)], ds_in.at[lax.rem(i, 2)], ds_sem.at[lax.rem(i, 2)])

    load_ds(0).start()

    def slice_of_work(i, _):
        @pl.when(i + 1 < SLICES)
        def _():
            load_ds(i + 1).start()
        load_ds(i).wait()
        c, k = i // QUARTERS, lax.rem(i, QUARTERS)

        @pl.when(k == 0)
        def _():
            qg_t[...] = jnp.zeros_like(qg_t)
        qg_t[...] += jnp.dot(keys_t[:, pl.ds(pl.multiple_of(k * BIG, BIG), BIG)], ds_in[lax.rem(i, 2)], preferred_element_type=jnp.float32)

        @pl.when(k == QUARTERS - 1)
        def _():
            row = pl.multiple_of((c // 2) * RUN, RUN)
            for h in range(0, GROUP, 2):
                a = qg_t[:, h * RUN:h * RUN + 2 * RUN].T.astype(jnp.bfloat16)
                lane = pl.multiple_of(lax.rem(c, 2) * (GROUP * KVW) + h * KVW, 128)
                qg_out[pl.ds(row, RUN), pl.ds(lane, 2 * KVW)] = jnp.concatenate([a[:RUN], a[RUN:]], axis=1)
        return 0

    done_work = [0]

    def work(n):
        first = done_work[0]
        done_work[0] += n
        lax.fori_loop(first, first + n, slice_of_work, 0)

    greet(place, core)
    count = [0]
    sent = []

    def copy(src, dst, dev):
        i = count[0]
        count[0] += 1
        c = pltpu.make_async_remote_copy(src, dst, send.at[i], recv.at[i], device_id=dev, device_id_type=MESH)
        c.start()
        sent.append(c)
        return c

    sibling = device(place, 1 - core)
    swaps, loads = [], []
    for n, (order, lane, width) in enumerate(PARTS):
        other = part_ref.at[:, :, :, pl.ds(32 * (1 - core), 32), pl.ds(lane, width)]
        swaps.append(copy(other, theirs[n], sibling))
        load = pltpu.make_async_copy(part_ref.at[:, :, :, pl.ds(32 * core, 32), pl.ds(lane, width)], mine[n], sem.at[n])
        load.start()
        loads.append(load)

    load_kt.wait()
    work(PLAN[0])
    halves = ((0, 16), (16, 16))
    for phase in range(3):
        started = []
        for n, (order, lane, width) in enumerate(PARTS):
            axis, done = order[phase], order[:phase]
            dim = dropped(axis, done)
            k, w, rl, ld = keep[n][phase], wire[n][phase], relay[n][phase], landed[n][phase]
            me = place[axis]
            right, left, opp = (lax.rem(me + i, 4) for i in (1, 3, 2))
            rdev, ldev = device(moved(place, axis, 1), core), device(moved(place, axis, 3), core)
            if phase == 0:
                loads[n].wait()
                swaps[n].wait_recv()
                def fill(v):
                    at(k, dim, v)[...] = at(mine[n], dim, v)[...].astype(jnp.float32) + at(theirs[n], dim, v)[...].astype(jnp.float32)
            else:
                def fill(v):
                    pass
            fill(opp)
            at(w, dim, opp)[...] = at(k, dim, opp)[...].astype(w.dtype)
            c0 = copy(at(w, dim, opp, halves[0]), rl.at[0], rdev)
            c1 = copy(at(w, dim, opp, halves[1]), rl.at[1], ldev)
            fill(right)
            at(w, dim, right, halves[1])[...] = at(k, dim, right, halves[1])[...].astype(w.dtype)
            c2 = copy(at(w, dim, right, halves[1]), ld.at[0, 1], rdev)
            fill(left)
            at(w, dim, left, halves[0])[...] = at(k, dim, left, halves[0])[...].astype(w.dtype)
            c3 = copy(at(w, dim, left, halves[0]), ld.at[1, 0], ldev)
            fill(me)
            started.append((c0, c1, c2, c3))
        work(PLAN[1 + 2 * phase])
        ended = []
        for n, (order, lane, width) in enumerate(PARTS):
            axis, done = order[phase], order[:phase]
            dim = dropped(axis, done)
            k, w, rl, ld = keep[n][phase], wire[n][phase], relay[n][phase], landed[n][phase]
            me = place[axis]
            right, left = lax.rem(me + 1, 4), lax.rem(me + 3, 4)
            rdev, ldev = device(moved(place, axis, 1), core), device(moved(place, axis, 3), core)
            c0, c1, c2, c3 = started[n]
            c0.wait_recv()
            at(w, dim, right, halves[0])[...] = (at(k, dim, right, halves[0])[...] + rl[0].astype(jnp.float32)).astype(w.dtype)
            c4 = copy(at(w, dim, right, halves[0]), ld.at[0, 0], rdev)
            c1.wait_recv()
            at(w, dim, left, halves[1])[...] = (at(k, dim, left, halves[1])[...] + rl[1].astype(jnp.float32)).astype(w.dtype)
            c5 = copy(at(w, dim, left, halves[1]), ld.at[1, 1], ldev)
            ended.append((c2, c3, c4, c5))
        work(PLAN[2 + 2 * phase])
        if phase == 2:
            put = pltpu.make_async_copy(qg_out, qg_ref, qg_sem)
            put.start()
        for n, (order, lane, width) in enumerate(PARTS):
            axis, done = order[phase], order[:phase]
            dim = dropped(axis, done)
            k, ld = keep[n][phase], landed[n][phase]
            for c in ended[n]:
                c.wait_recv()
            for h in (0, 1):
                total = (at(k, dim, place[axis], halves[h])[...] + ld[0, h].astype(jnp.float32)) + ld[1, h].astype(jnp.float32)
                if phase < 2:
                    to = keep[n][phase + 1]
                    to.at[tuple([slice(None)] * (2 - phase) + [pl.ds(*halves[h])])][...] = total
                else:
                    real = min(width, KVW - lane)
                    out_ref[pl.ds(*halves[h]), pl.ds(lane, real)] = total[:, :real]
    put.wait()
    for s in sent:
        s.wait_send()


N_SCATTER = 3 + 9 * 6
WIRES = (jnp.bfloat16, jnp.float32, jnp.float32)


def scatter(part, ds, keys_t):
    V, f32, bf16 = pltpu.VMEM, jnp.float32, jnp.bfloat16
    mine = [V((4, 4, 4, 32, w), bf16) for _, _, w in PARTS]
    keep = [[V((4,) * (3 - p) + (32, w), f32) for p in range(3)] for _, _, w in PARTS]
    wire = [[V((4,) * (3 - p) + (32, w), WIRES[p]) for p in range(3)] for _, _, w in PARTS]
    relay = [[V((2,) + (4,) * (2 - p) + (16, w), WIRES[p]) for p in range(3)] for _, _, w in PARTS]
    landed = [[V((2, 2) + (4,) * (2 - p) + (16, w), WIRES[p]) for p in range(3)] for _, _, w in PARTS]
    return pl.pallas_call(
        scatter_kernel,
        out_shape=(jax.ShapeDtypeStruct((32, KVW), f32), jax.ShapeDtypeStruct((2 * RUN, HEADS * KVW), bf16)),
        in_specs=[pl.BlockSpec(memory_space=pltpu.HBM)] * 3,
        out_specs=(pl.BlockSpec(memory_space=pltpu.VMEM), pl.BlockSpec(memory_space=pltpu.HBM)),
        scratch_shapes=[
            mine, list(mine), keep, wire, relay, landed,
            V((KVW, TOKENS), bf16), V((2, BIG, ROWS), bf16), V((KVW, ROWS), f32), V((2 * RUN, HEADS * KVW), bf16),
            pltpu.SemaphoreType.DMA((3,)), pltpu.SemaphoreType.DMA, pltpu.SemaphoreType.DMA((2,)), pltpu.SemaphoreType.DMA,
            pltpu.SemaphoreType.DMA((N_SCATTER,)),
            pltpu.SemaphoreType.DMA((N_SCATTER,)),
        ],
        compiler_params=pltpu.CompilerParams(collective_id=1, has_side_effects=True, vmem_limit_bytes=56 * 2**20),
        cost_estimate=pl.CostEstimate(flops=10**10, bytes_accessed=3 * 10**7, transcendentals=0),
        name="scatter_latent_grad",
    )(part, ds, keys_t)


def attend_kernel(pos_ref, q_ref, do_ref, kg_ref, ds_ref, kt_ref, part_ref,
                  chip_run, chip_of, keys, keys_t, acc, exps, gws, tops, qs, qs_t, dos, dos_t, q_in, do_in, ds_out, zeros,
                  tags, tags_i, key_sem, in_sem, out_sem, ds_sem, zero_sem):
    f32, bf16 = jnp.float32, jnp.bfloat16
    copy_q = pltpu.make_async_copy(q_ref, q_in, in_sem.at[0])
    copy_do = pltpu.make_async_copy(do_ref, do_in, in_sem.at[1])
    copy_tags = pltpu.make_async_copy(kg_ref.at[0, :, pl.ds(0, 16), pl.ds(LAT, 128)], tags, in_sem.at[2])
    copy_tags.start()
    copy_q.start()
    copy_do.start()
    zeros[...] = jnp.zeros_like(zeros)
    copy_tags.wait()
    tags_i[...] = tags[:, 0, :].astype(f32).astype(jnp.int32)
    move_tags = pltpu.make_async_copy(tags_i, chip_run, in_sem.at[2])
    move_tags.start()
    acc[...] = jnp.zeros_like(acc)
    move_tags.wait()

    def place(chip, _):
        run = chip_run[chip, KVW - LAT]
        chip_of[run] = chip
        for c in range(2):
            pltpu.make_async_copy(kg_ref.at[c, chip], keys.at[pl.ds(run * RUN + c * 32, 32)], key_sem).start()
        return 0

    lax.fori_loop(0, RUNS, place, 0)
    qs[:, LAT:] = jnp.zeros((ROWS, PAD - LAT), bf16)
    pltpu.make_async_copy(keys, keys, key_sem).wait()

    def turn(j, _):
        o = pl.multiple_of(j * 256, 256)
        keys_t[:, pl.ds(o, 256)] = keys[pl.ds(o, 256), :KVW].T
        return 0

    lax.fori_loop(0, TOKENS // 256, turn, 0)
    copy_kt = pltpu.make_async_copy(keys_t, kt_ref, in_sem.at[2])
    copy_kt.start()
    copy_q.wait()
    copy_do.wait()

    def chunk(c, made):
        half, block = lax.rem(c, 2), c // 2
        run = pos_ref[block * RUN] // RUN
        row = pl.multiple_of(block * RUN, RUN)
        for h in range(0, GROUP, 2):
            v = q_in[pl.ds(row, RUN), pl.ds(pl.multiple_of(half * (GROUP * KVW) + h * KVW, 128), 2 * KVW)]
            qs[h * RUN:h * RUN + RUN, :KVW] = v[:, :KVW]
            qs[h * RUN + RUN:h * RUN + 2 * RUN, :KVW] = v[:, KVW:]
            d = do_in[pl.ds(row, RUN), pl.ds(pl.multiple_of(half * (GROUP * LAT) + h * LAT, 128), 2 * LAT)]
            dos[h * RUN:h * RUN + RUN, :] = d[:, :LAT]
            dos[h * RUN + RUN:h * RUN + 2 * RUN, :] = d[:, LAT:]
        qs_t[...] = qs[...].T
        dos_t[...] = dos[...].T
        small = run // (SMALL // RUN)
        bulk = small // 2
        odd = lax.rem(small, 2) == 1

        def scan(t, size, masked, carry):
            m, l, d = carry
            o = pl.multiple_of(t * BIG, BIG)
            tile = keys[pl.ds(o, size), :]
            s = jnp.dot(tile, qs_t[...], preferred_element_type=f32)
            g = jnp.dot(tile[:, :LAT], dos_t[...], preferred_element_type=f32)
            if masked:
                key = lax.broadcasted_iota(jnp.int32, (size, ROWS), 0)
                tok = lax.broadcasted_iota(jnp.int32, (size, ROWS), 1) % RUN
                s = jnp.where(key - tok <= run * RUN - o, s, MASKED)
            s = s * TO_BASE_2
            top = jnp.maximum(m, jnp.max(s, axis=0, keepdims=True))
            e = jnp.exp2(s - top)
            exps[pl.ds(o, size), :] = e
            gws[pl.ds(o, size), :] = g
            tops[pl.ds(t * 8, 8), :] = jnp.broadcast_to(top, (8, ROWS))
            a = jnp.exp2(m - top)
            return top, l * a + jnp.sum(e, axis=0, keepdims=True), d * a + jnp.sum(e * g, axis=0, keepdims=True)

        start = (jnp.full((1, ROWS), MASKED, f32), jnp.zeros((1, ROWS), f32), jnp.zeros((1, ROWS), f32))
        carry = lax.fori_loop(0, bulk, lambda t, s: scan(t, BIG, False, s), start)
        m, l, d = lax.cond(odd, lambda: scan(bulk, BIG, True, carry), lambda: scan(bulk, SMALL, True, carry))
        share = 1.0 / l
        delta = d * share

        def leave_ds(slot, t):
            return pltpu.make_async_copy(ds_out.at[slot], ds_ref.at[c, pl.ds(t * BIG, BIG)], ds_sem.at[slot])

        def back(t, size):
            n = made + t
            slot = lax.rem(n, 2)

            @pl.when(n >= 2)
            def _():
                leave_ds(slot, t).wait()
            o = pl.multiple_of(t * BIG, BIG)
            span = pl.ds(o, size)
            w = exps[span, :] * (jnp.exp2(tops[pl.ds(t * 8, 8), :][:1] - m) * share)
            ds = (w * ((gws[span, :] - delta) * SCALE)).astype(bf16)
            ds_out[slot, :size] = ds
            if size < BIG:
                ds_out[slot, size:] = jnp.zeros((BIG - size, ROWS), bf16)
            leave_ds(slot, t).start()
            nt = (((1,), (1,)), ((), ()))
            acc[:LAT, span] += (lax.dot_general(qs_t[:LAT], ds, nt, preferred_element_type=f32)
                                + lax.dot_general(dos_t[...], w.astype(bf16), nt, preferred_element_type=f32))
            acc[LAT:, span] += lax.dot_general(qs_t[LAT:KVW], ds, nt, preferred_element_type=f32)

        def bulk_back(t, _):
            back(t, BIG)
            return 0

        lax.fori_loop(0, bulk, bulk_back, 0)
        pl.when(odd)(lambda: back(bulk, BIG))
        pl.when(jnp.logical_not(odd))(lambda: back(bulk, SMALL))

        def blank(t, _):
            pltpu.make_async_copy(zeros, ds_ref.at[c, pl.ds(t * BIG, BIG)], zero_sem).start()
            return 0

        lax.fori_loop(bulk + 1, QUARTERS, blank, 0)
        return made + bulk + 1

    made = lax.fori_loop(0, CHUNKS, chunk, 0)

    def leave(j, _):
        o = pl.multiple_of(j * 256, 256)
        keys[pl.ds(o, 256), :KVW] = acc[:, pl.ds(o, 256)].astype(bf16).T
        for i in range(4):
            pltpu.make_async_copy(keys.at[pl.ds(o + i * RUN, RUN)], part_ref.at[chip_of[j * 4 + i]], out_sem).start()
        return 0

    lax.fori_loop(0, TOKENS // 256, leave, 0)
    copy_kt.wait()
    for slot in range(2):
        pltpu.make_async_copy(ds_out.at[slot], ds_ref.at[0, pl.ds(0, BIG)], ds_sem.at[slot]).wait()

    def blanked(i, _):
        pltpu.make_async_copy(zeros, ds_ref.at[0, pl.ds(0, BIG)], zero_sem).wait()
        return 0

    lax.fori_loop(made, SLICES, blanked, 0)
    pltpu.make_async_copy(keys, keys, out_sem).wait()


def attend(positions, query, out_grad, gathered):
    V, f32, bf16 = pltpu.VMEM, jnp.float32, jnp.bfloat16
    return pl.pallas_call(
        attend_kernel,
        out_shape=(jax.ShapeDtypeStruct((CHUNKS, TOKENS, ROWS), bf16), jax.ShapeDtypeStruct((KVW, TOKENS), bf16),
                   jax.ShapeDtypeStruct((RUNS, RUN, PAD), bf16)),
        in_specs=[pl.BlockSpec(memory_space=pltpu.SMEM)] + [pl.BlockSpec(memory_space=pltpu.HBM)] * 3,
        out_specs=(pl.BlockSpec(memory_space=pltpu.HBM),) * 3,
        scratch_shapes=[
            pltpu.SMEM((RUNS, 128), jnp.int32), pltpu.SMEM((RUNS,), jnp.int32),
            V((TOKENS, PAD), bf16), V((KVW, TOKENS), bf16), V((KVW, TOKENS), f32),
            V((TOKENS, ROWS), f32), V((TOKENS, ROWS), f32), V((QUARTERS * 8, ROWS), f32),
            V((ROWS, PAD), bf16), V((PAD, ROWS), bf16), V((ROWS, LAT), bf16), V((LAT, ROWS), bf16),
            V((2 * RUN, HEADS * KVW), bf16), V((2 * RUN, HEADS * LAT), bf16), V((2, BIG, ROWS), bf16), V((BIG, ROWS), bf16),
            V((RUNS, 16, 128), bf16), V((RUNS, 128), jnp.int32),
            pltpu.SemaphoreType.DMA, pltpu.SemaphoreType.DMA((3,)), pltpu.SemaphoreType.DMA, pltpu.SemaphoreType.DMA((2,)),
            pltpu.SemaphoreType.DMA,
        ],
        compiler_params=pltpu.CompilerParams(vmem_limit_bytes=60 * 2**20),
        cost_estimate=pl.CostEstimate(flops=46 * 10**9, bytes_accessed=2 * 10**7, transcendentals=10**7),
        name="attend",
    )(positions, query, out_grad, gathered)


def per_device(query, latent, out_grad, positions):
    gathered = gather(positions, latent)
    ds, keys_t, part = attend(positions, query, out_grad, gathered.reshape(2, RUNS, 32, PAD))
    latent_grad, query_grad = scatter(part.reshape(4, 4, 4, RUN, PAD), ds, keys_t)
    return query_grad, latent_grad


def solution(mesh):
    return jax.shard_map(
        per_device,
        mesh=mesh,
        in_specs=(P("seq", "tp"), P(("seq", "tp"), None), P("seq", "tp"), P("seq")),
        out_specs=(P("seq", "tp"), P(("seq", "tp"), None)),
        check_vma=False,
    )
```

```python
import math

import jax, jax.numpy as jnp
from jax import lax
from jax.experimental import pallas as pl
from jax.experimental.pallas import tpu as pltpu
from jax.sharding import PartitionSpec as P

LAT=512; KVW=576; PAD=640
SCALE = 192.0 ** -0.5
TO_BASE_2 = SCALE * math.log2(math.e)
MASKED = -1e30
TOKENS = 4096
RUN = 64
RUNS = TOKENS // RUN
HEADS = 16
GROUP = 8
ROWS = GROUP * RUN
HUGE, BIG, SMALL = 2048, 1024, 512
CHUNKS = 2 * HEADS // GROUP
QUARTERS = TOKENS // BIG
SLICES = CHUNKS * QUARTERS
PLAN = (4, 4, 3, 2, 1, 1, 1)
MESH = pl.DeviceIdType.MESH
PARTS = (((0, 1, 2), 0, 256), ((1, 2, 0), 256, 256), ((2, 0, 1), 512, 128))


def coords():
    seq, tp = lax.axis_index("seq"), lax.axis_index("tp")
    x = lax.rem(seq, 4)
    z = lax.rem(seq // 4, 2) * 2 + tp // 2
    y = seq // 8
    return [x, y, z], lax.rem(tp, 2)


def device(place, core):
    x, y, z = place
    return ((y * 2 + z // 2) * 4 + x, lax.rem(z, 2) * 2 + core)


def moved(place, axis, by):
    out = list(place)
    out[axis] = lax.rem(place[axis] + by, 4)
    return out


def greet(place, core, opposite=False):
    barrier = pltpu.get_barrier_semaphore()
    steps = (1, 2, 3) if opposite else (1, 3)
    for axis in range(3):
        for by in steps:
            pl.semaphore_signal(barrier, inc=1, device_id=device(moved(place, axis, by), core), device_id_type=MESH)
    pl.semaphore_signal(barrier, inc=1, device_id=device(place, 1 - core), device_id_type=MESH)
    pl.semaphore_wait(barrier, 3 * len(steps) + 1)


def gather_kernel(pos_ref, lat_ref, out_ref, runs_ref, own, tags, tags_f, sem, send, recv):
    place, core = coords()
    run = pos_ref[lax.rem(place[2], 2) * 64] // 64
    own[:, :KVW] = lat_ref[...]
    own[:, KVW:] = jnp.full((32, PAD - KVW), run.astype(jnp.float32)).astype(jnp.bfloat16)
    put = pltpu.make_async_copy(own, out_ref.at[place[0], place[1], place[2], core], sem)
    put.start()
    greet(place, core, True)
    put.wait()
    sent = []

    def copy(ref, dev):
        i = len(sent)
        c = pltpu.make_async_remote_copy(ref, ref, send.at[i], recv.at[i], device_id=dev, device_id_type=MESH)
        c.start()
        sent.append(c)
        return c

    def shards(order, lane, width, at1, at2, at3, rows=(0, 32)):
        at = [None] * 3
        for axis, v in zip(order, (at1, at2, at3)):
            at[axis] = pl.ds(0, 4) if v is None else lax.rem(place[axis] + v, 4)
        return out_ref.at[at[0], at[1], at[2], core, pl.ds(*rows), pl.ds(lane, width)]

    sibling = device(place, 1 - core)
    twins = []
    one, two, three = {}, {}, {}
    steps = (1, 3, 2)

    def spread(p, d1):
        order, lane, width = PARTS[p]
        for by in steps:
            two[p, d1, by] = copy(shards(order, lane, width, d1, 0, 0), device(moved(place, order[1], by), core))

    def shift(p, d2):
        order, lane, width = PARTS[p]
        for by in (1, 3):
            three[p, d2, by] = copy(shards(order, lane, width, None, d2, 0), device(moved(place, order[2], by), core))

    def forward(p, d2):
        order, lane, width = PARTS[p]
        three[p, d2, 1].wait_recv()
        three[p, d2, 4] = copy(shards(order, lane, width, None, d2, 3, (0, 16)), device(moved(place, order[2], 1), core))
        three[p, d2, 3].wait_recv()
        three[p, d2, 5] = copy(shards(order, lane, width, None, d2, 1, (16, 16)), device(moved(place, order[2], 3), core))

    def arrive(p, d2):
        for d1 in (0, 1, 3, 2):
            two[p, d1, {3: 1, 1: 3, 2: 2}[d2]].wait_recv()

    n = range(len(PARTS))
    for p in n:
        order, lane, width = PARTS[p]
        for by in steps:
            one[p, by] = copy(shards(order, lane, width, 0, 0, 0), device(moved(place, order[0], by), core))
    for p in n:
        spread(p, 0)
    for by in steps:
        for p in n:
            one[p, by].wait_recv()
            spread(p, {1: 3, 3: 1, 2: 2}[by])
    for p in n:
        shift(p, 0)
    for d2 in (3, 1, 2):
        for p in n:
            arrive(p, d2)
            shift(p, d2)
    for p in n:
        order, lane, width = PARTS[p]
        twins.append(copy(shards(order, lane, width, None, None, 0), sibling))
    for d2 in (0, 3, 1, 2):
        for p in n:
            forward(p, d2)
    for p in n:
        order, lane, width = PARTS[p]
        twins.append(copy(shards(order, lane, width, None, None, 3), sibling))
        twins.append(copy(shards(order, lane, width, None, None, 1), sibling))
    for p in (2, 0, 1):
        order, lane, width = PARTS[p]
        for d2 in (0, 3, 1, 2):
            three[p, d2, 4].wait_recv()
            three[p, d2, 5].wait_recv()
            twins.append(copy(shards(order, lane, width, None, d2, 2), sibling))
        if p == 2:
            load_tags = pltpu.make_async_copy(out_ref.at[:, :, :, core, pl.ds(0, 16), pl.ds(LAT, 128)], tags, sem)
            load_tags.start()
    load_tags.wait()
    tags_f[...] = jnp.zeros_like(tags_f)
    tags_f[:RUNS, :] = tags[:, :, :, 0, :].reshape(RUNS, 128).astype(jnp.float32)
    runs_ref[...] = tags_f[...].T[KVW - LAT:KVW - LAT + 8, :].astype(jnp.int32)
    for t in twins:
        t.wait_recv()
    for s in sent:
        s.wait_send()


N_GATHER = 3 * (3 + 12 + 8 + 1 + 8 + 2 + 4)


def gather(positions, latent):
    return pl.pallas_call(
        gather_kernel,
        out_shape=(jax.ShapeDtypeStruct((4, 4, 4, 2, 32, PAD), jnp.bfloat16), jax.ShapeDtypeStruct((8, 128), jnp.int32)),
        in_specs=[pl.BlockSpec(memory_space=pltpu.SMEM), pl.BlockSpec(memory_space=pltpu.VMEM)],
        out_specs=(pl.BlockSpec(memory_space=pltpu.HBM), pl.BlockSpec(memory_space=pltpu.VMEM)),
        scratch_shapes=[
            pltpu.VMEM((32, PAD), jnp.bfloat16),
            pltpu.VMEM((4, 4, 4, 16, 128), jnp.bfloat16),
            pltpu.VMEM((128, 128), jnp.float32),
            pltpu.SemaphoreType.DMA,
            pltpu.SemaphoreType.DMA((N_GATHER,)),
            pltpu.SemaphoreType.DMA((N_GATHER,)),
        ],
        compiler_params=pltpu.CompilerParams(collective_id=0, has_side_effects=True),
        cost_estimate=pl.CostEstimate(flops=0, bytes_accessed=10 * 2**20, transcendentals=0),
        name="gather_latent",
    )(positions, latent)


def dropped(axis, done):
    return axis - sum(1 for a in done if a < axis)


def at(ref, dim, value, rows=None):
    index = [slice(None)] * dim + [value]
    view = ref.at[tuple(index)]
    if rows is not None:
        lead = len(view.shape) - 2
        view = view.at[tuple([slice(None)] * lead + [pl.ds(*rows)])]
    return view


def scatter_kernel(part_ref, ds_ref, keys_ref, out_ref, qg_ref, mine, theirs, keep, wire, relay, landed,
                   keys, keys_t, ds_in, qg_t, qg_out, sem, kt_sem, ds_sem, qg_sem, send, recv):
    place, core = coords()
    load_keys = pltpu.make_async_copy(keys_ref, keys, kt_sem)
    load_keys.start()

    def load_ds(i):
        return pltpu.make_async_copy(ds_ref.at[i // QUARTERS, pl.ds(lax.rem(i, QUARTERS) * BIG, BIG)], ds_in.at[lax.rem(i, 2)], ds_sem.at[lax.rem(i, 2)])

    load_ds(0).start()

    def slice_of_work(i, _):
        @pl.when(i + 1 < SLICES)
        def _():
            load_ds(i + 1).start()
        load_ds(i).wait()
        c, k = i // QUARTERS, lax.rem(i, QUARTERS)

        @pl.when(k == 0)
        def _():
            qg_t[...] = jnp.zeros_like(qg_t)
        qg_t[...] += jnp.dot(keys_t[:, pl.ds(pl.multiple_of(k * BIG, BIG), BIG)], ds_in[lax.rem(i, 2)], preferred_element_type=jnp.float32)

        @pl.when(k == QUARTERS - 1)
        def _():
            row = pl.multiple_of((c // 2) * RUN, RUN)
            for h in range(0, GROUP, 2):
                a = qg_t[:, h * RUN:h * RUN + 2 * RUN].T.astype(jnp.bfloat16)
                lane = pl.multiple_of(lax.rem(c, 2) * (GROUP * KVW) + h * KVW, 128)
                qg_out[pl.ds(row, RUN), pl.ds(lane, 2 * KVW)] = jnp.concatenate([a[:RUN], a[RUN:]], axis=1)
        return 0

    done_work = [0]

    def work(n):
        first = done_work[0]
        done_work[0] += n
        lax.fori_loop(first, first + n, slice_of_work, 0)

    greet(place, core)
    count = [0]
    sent = []

    def copy(src, dst, dev):
        i = count[0]
        count[0] += 1
        c = pltpu.make_async_remote_copy(src, dst, send.at[i], recv.at[i], device_id=dev, device_id_type=MESH)
        c.start()
        sent.append(c)
        return c

    sibling = device(place, 1 - core)
    swaps, loads = [], []
    for n, (order, lane, width) in enumerate(PARTS):
        other = part_ref.at[:, :, :, pl.ds(32 * (1 - core), 32), pl.ds(lane, width)]
        swaps.append(copy(other, theirs[n], sibling))
        load = pltpu.make_async_copy(part_ref.at[:, :, :, pl.ds(32 * core, 32), pl.ds(lane, width)], mine[n], sem.at[n])
        load.start()
        loads.append(load)

    load_keys.wait()

    def turn(j, _):
        o = pl.multiple_of(j * 256, 256)
        keys_t[:, pl.ds(o, 256)] = keys[pl.ds(o, 256), :KVW].T
        return 0

    lax.fori_loop(0, TOKENS // 256, turn, 0)
    work(PLAN[0])
    halves = ((0, 16), (16, 16))
    for phase in range(3):
        started = []
        for n, (order, lane, width) in enumerate(PARTS):
            axis, done = order[phase], order[:phase]
            dim = dropped(axis, done)
            k, w, rl, ld = keep[n][phase], wire[n][phase], relay[n][phase], landed[n][phase]
            me = place[axis]
            right, left, opp = (lax.rem(me + i, 4) for i in (1, 3, 2))
            rdev, ldev = device(moved(place, axis, 1), core), device(moved(place, axis, 3), core)
            if phase == 0:
                loads[n].wait()
                swaps[n].wait_recv()
                def fill(v):
                    at(k, dim, v)[...] = at(mine[n], dim, v)[...].astype(jnp.float32) + at(theirs[n], dim, v)[...].astype(jnp.float32)
            else:
                def fill(v):
                    pass
            fill(opp)
            at(w, dim, opp)[...] = at(k, dim, opp)[...].astype(w.dtype)
            c0 = copy(at(w, dim, opp, halves[0]), rl.at[0], rdev)
            c1 = copy(at(w, dim, opp, halves[1]), rl.at[1], ldev)
            fill(right)
            at(w, dim, right, halves[1])[...] = at(k, dim, right, halves[1])[...].astype(w.dtype)
            c2 = copy(at(w, dim, right, halves[1]), ld.at[0, 1], rdev)
            fill(left)
            at(w, dim, left, halves[0])[...] = at(k, dim, left, halves[0])[...].astype(w.dtype)
            c3 = copy(at(w, dim, left, halves[0]), ld.at[1, 0], ldev)
            fill(me)
            started.append((c0, c1, c2, c3))
        work(PLAN[1 + 2 * phase])
        ended = []
        for n, (order, lane, width) in enumerate(PARTS):
            axis, done = order[phase], order[:phase]
            dim = dropped(axis, done)
            k, w, rl, ld = keep[n][phase], wire[n][phase], relay[n][phase], landed[n][phase]
            me = place[axis]
            right, left = lax.rem(me + 1, 4), lax.rem(me + 3, 4)
            rdev, ldev = device(moved(place, axis, 1), core), device(moved(place, axis, 3), core)
            c0, c1, c2, c3 = started[n]
            c0.wait_recv()
            at(w, dim, right, halves[0])[...] = (at(k, dim, right, halves[0])[...] + rl[0].astype(jnp.float32)).astype(w.dtype)
            c4 = copy(at(w, dim, right, halves[0]), ld.at[0, 0], rdev)
            c1.wait_recv()
            at(w, dim, left, halves[1])[...] = (at(k, dim, left, halves[1])[...] + rl[1].astype(jnp.float32)).astype(w.dtype)
            c5 = copy(at(w, dim, left, halves[1]), ld.at[1, 1], ldev)
            ended.append((c2, c3, c4, c5))
        work(PLAN[2 + 2 * phase])
        if phase == 2:
            put = pltpu.make_async_copy(qg_out, qg_ref, qg_sem)
            put.start()
        for n, (order, lane, width) in enumerate(PARTS):
            axis, done = order[phase], order[:phase]
            dim = dropped(axis, done)
            k, ld = keep[n][phase], landed[n][phase]
            for c in ended[n]:
                c.wait_recv()
            for h in (0, 1):
                total = (at(k, dim, place[axis], halves[h])[...] + ld[0, h].astype(jnp.float32)) + ld[1, h].astype(jnp.float32)
                if phase < 2:
                    to = keep[n][phase + 1]
                    to.at[tuple([slice(None)] * (2 - phase) + [pl.ds(*halves[h])])][...] = total
                else:
                    real = min(width, KVW - lane)
                    out_ref[pl.ds(*halves[h]), pl.ds(lane, real)] = total[:, :real]
    put.wait()
    for s in sent:
        s.wait_send()


N_SCATTER = 3 + 9 * 6
WIRES = (jnp.bfloat16, jnp.float32, jnp.float32)


def scatter(part, ds, keys):
    V, f32, bf16 = pltpu.VMEM, jnp.float32, jnp.bfloat16
    mine = [V((4, 4, 4, 32, w), bf16) for _, _, w in PARTS]
    keep = [[V((4,) * (3 - p) + (32, w), f32) for p in range(3)] for _, _, w in PARTS]
    wire = [[V((4,) * (3 - p) + (32, w), WIRES[p]) for p in range(3)] for _, _, w in PARTS]
    relay = [[V((2,) + (4,) * (2 - p) + (16, w), WIRES[p]) for p in range(3)] for _, _, w in PARTS]
    landed = [[V((2, 2) + (4,) * (2 - p) + (16, w), WIRES[p]) for p in range(3)] for _, _, w in PARTS]
    return pl.pallas_call(
        scatter_kernel,
        out_shape=(jax.ShapeDtypeStruct((32, KVW), f32), jax.ShapeDtypeStruct((2 * RUN, HEADS * KVW), bf16)),
        in_specs=[pl.BlockSpec(memory_space=pltpu.HBM)] * 3,
        out_specs=(pl.BlockSpec(memory_space=pltpu.VMEM), pl.BlockSpec(memory_space=pltpu.HBM)),
        scratch_shapes=[
            mine, list(mine), keep, wire, relay, landed,
            V((TOKENS, PAD), bf16), V((KVW, TOKENS), bf16), V((2, BIG, ROWS), bf16), V((KVW, ROWS), f32), V((2 * RUN, HEADS * KVW), bf16),
            pltpu.SemaphoreType.DMA((3,)), pltpu.SemaphoreType.DMA, pltpu.SemaphoreType.DMA((2,)), pltpu.SemaphoreType.DMA,
            pltpu.SemaphoreType.DMA((N_SCATTER,)),
            pltpu.SemaphoreType.DMA((N_SCATTER,)),
        ],
        compiler_params=pltpu.CompilerParams(collective_id=1, has_side_effects=True, vmem_limit_bytes=56 * 2**20),
        cost_estimate=pl.CostEstimate(flops=10**10, bytes_accessed=3 * 10**7, transcendentals=0),
        name="scatter_latent_grad",
    )(part, ds, keys)


def attend_kernel(pos_ref, runs_ref, q_ref, do_ref, kg_ref, ds_ref, keys_ref, part_ref,
                  chip_of, keys, acc, exps, gws, tops, qs, qs_t, dos, dos_t, q_in, do_in, ds_out,
                  key_sem, in_sem, out_sem, ds_sem):
    f32, bf16 = jnp.float32, jnp.bfloat16
    copy_keys = pltpu.make_async_copy(keys, keys_ref, out_sem.at[1])

    def inputs(c):
        row = pl.ds(pl.multiple_of((c // 2) * RUN, RUN), RUN)
        out = []
        for i, (ref, to, width) in enumerate(((q_ref, q_in, GROUP * KVW), (do_ref, do_in, GROUP * LAT))):
            lane = pl.ds(pl.multiple_of(lax.rem(c, 2) * width, 128), width)
            out.append(pltpu.make_async_copy(ref.at[row, lane], to.at[row, lane], in_sem.at[i, c]))
        return out

    def take(c, _):
        for copy in inputs(c):
            copy.start()
        return 0

    take(0, 0)

    def place(chip, _):
        chip_of[runs_ref[0, chip]] = chip
        return 0

    lax.fori_loop(0, RUNS, place, 0)

    def fetch(j, _):
        pltpu.make_async_copy(kg_ref.at[chip_of[j]], keys.at[pl.ds(j * RUN, RUN)], key_sem.at[j // (BIG // RUN)]).start()
        return 0

    lax.fori_loop(0, BIG // RUN, fetch, 0)
    lax.fori_loop(BIG // RUN, RUNS, fetch, 0)
    lax.fori_loop(1, CHUNKS, take, 0)

    def await_keys(t, _):
        tile = keys.at[pl.ds(pl.multiple_of(t * BIG, BIG), BIG)]
        pltpu.make_async_copy(tile, tile, key_sem.at[t]).wait()
        return 0

    acc[...] = jnp.zeros_like(acc)
    qs[:, LAT:] = jnp.zeros((ROWS, PAD - LAT), bf16)

    def chunk(c, _):
        for copy in inputs(c):
            copy.wait()
        half, block, slot = lax.rem(c, 2), c // 2, lax.rem(c, 2)
        run = pos_ref[block * RUN] // RUN
        row = pl.multiple_of(block * RUN, RUN)
        for h in range(0, GROUP, 2):
            v = q_in[pl.ds(row, RUN), pl.ds(pl.multiple_of(half * (GROUP * KVW) + h * KVW, 128), 2 * KVW)]
            qs[h * RUN:h * RUN + RUN, :KVW] = v[:, :KVW]
            qs[h * RUN + RUN:h * RUN + 2 * RUN, :KVW] = v[:, KVW:]
            d = do_in[pl.ds(row, RUN), pl.ds(pl.multiple_of(half * (GROUP * LAT) + h * LAT, 128), 2 * LAT)]
            dos[h * RUN:h * RUN + RUN, :] = d[:, :LAT]
            dos[h * RUN + RUN:h * RUN + 2 * RUN, :] = d[:, LAT:]
        qs_t[...] = qs[...].T
        dos_t[...] = dos[...].T
        full = run // (SMALL // RUN)
        huge = full // 4
        rest = lax.rem(full, 4)
        big = rest // 2
        odd = lax.rem(rest, 2) == 1
        last = huge * 4 + big * 2

        def scan(u, size, masked, carry):
            m, l, d = carry

            @pl.when(c == 0)
            def _():
                for i in range(max(size // BIG, 1)):
                    await_keys(u // 2 + i, 0)
            o = pl.multiple_of(u * SMALL, SMALL)
            tile = keys[pl.ds(o, size), :]
            s = jnp.dot(tile, qs_t[...], preferred_element_type=f32)
            g = jnp.dot(tile[:, :LAT], dos_t[...], preferred_element_type=f32)
            if masked:
                key = lax.broadcasted_iota(jnp.int32, (size, ROWS), 0)
                tok = lax.broadcasted_iota(jnp.int32, (size, ROWS), 1) % RUN
                s = jnp.where(key - tok <= run * RUN - o, s, MASKED)
            s = s * TO_BASE_2
            top = jnp.maximum(m, jnp.max(s, axis=0, keepdims=True))
            e = jnp.exp2(s - top)
            exps[pl.ds(o, size), :] = e
            gws[pl.ds(o, size), :] = g
            tops[pl.ds(pl.multiple_of(u * 8, 8), 8), :] = jnp.broadcast_to(top, (8, ROWS))
            a = jnp.exp2(m - top)
            return top, l * a + jnp.sum(e, axis=0, keepdims=True), d * a + jnp.sum(e * g, axis=0, keepdims=True)

        start = (jnp.full((1, ROWS), MASKED, f32), jnp.zeros((1, ROWS), f32), jnp.zeros((1, ROWS), f32))
        carry = lax.fori_loop(0, huge, lambda t, s: scan(t * 4, HUGE, False, s), start)
        carry = lax.fori_loop(0, big, lambda t, s: scan(huge * 4, BIG, False, s), carry)
        m, l, d = lax.cond(odd, lambda: scan(last, BIG, True, carry), lambda: scan(last, SMALL, True, carry))

        @pl.when(c == 0)
        def _():
            lax.fori_loop(last // 2 + 1, TOKENS // BIG, await_keys, 0)
            copy_keys.start()
        share = 1.0 / l
        delta = d * share

        @pl.when(c >= 2)
        def _():
            pltpu.make_async_copy(ds_out.at[slot], ds_ref.at[c], ds_sem.at[slot]).wait()

        def leave_ds(k, _):
            span = pl.ds(pl.multiple_of(k * BIG, BIG), BIG)
            pltpu.make_async_copy(ds_out.at[slot, span], ds_ref.at[c, span], ds_sem.at[slot]).start()
            return 0

        def back(u, size):
            o = pl.multiple_of(u * SMALL, SMALL)
            span = pl.ds(o, size)
            w = exps[span, :] * (jnp.exp2(tops[pl.ds(pl.multiple_of(u * 8, 8), 8), :][:1] - m) * share)
            ds = (w * ((gws[span, :] - delta) * SCALE)).astype(bf16)
            ds_out[slot, span, :] = ds
            nt = (((1,), (1,)), ((), ()))
            acc[:, span] += lax.dot_general(qs_t[:KVW], ds, nt, preferred_element_type=f32)
            acc[:LAT, span] += lax.dot_general(dos_t[...], w.astype(bf16), nt, preferred_element_type=f32)
            for k in range(max(size // BIG, 1)):
                leave_ds(u // 2 + k, 0)
            return 0

        def blank(u, _):
            ds_out[slot, pl.ds(pl.multiple_of(u * SMALL, SMALL), SMALL), :] = jnp.zeros((SMALL, ROWS), bf16)
            return 0

        lax.fori_loop(full + 1, TOKENS // SMALL, blank, 0)
        lax.fori_loop(last // 2 + 1, QUARTERS, leave_ds, 0)
        lax.fori_loop(0, huge, lambda t, _: back(t * 4, HUGE), 0)
        lax.fori_loop(0, big, lambda t, _: back(huge * 4, BIG), 0)

        @pl.when(odd)
        def _():
            back(last, BIG)

        @pl.when(jnp.logical_not(odd))
        def _():
            back(last, SMALL)

        return 0

    lax.fori_loop(0, CHUNKS, chunk, 0)
    copy_keys.wait()

    def leave(j, _):
        o = pl.multiple_of(j * 256, 256)
        keys[pl.ds(o, 256), :KVW] = acc[:, pl.ds(o, 256)].astype(bf16).T
        for i in range(4):
            pltpu.make_async_copy(keys.at[pl.ds(o + i * RUN, RUN)], part_ref.at[chip_of[j * 4 + i]], out_sem.at[0]).start()
        return 0

    lax.fori_loop(0, TOKENS // 256, leave, 0)
    for slot in range(2):
        pltpu.make_async_copy(ds_out.at[slot], ds_ref.at[0], ds_sem.at[slot]).wait()
    pltpu.make_async_copy(keys, keys, out_sem.at[0]).wait()


def attend(positions, runs, query, out_grad, gathered):
    V, f32, bf16 = pltpu.VMEM, jnp.float32, jnp.bfloat16
    return pl.pallas_call(
        attend_kernel,
        out_shape=(jax.ShapeDtypeStruct((CHUNKS, TOKENS, ROWS), bf16), jax.ShapeDtypeStruct((TOKENS, PAD), bf16),
                   jax.ShapeDtypeStruct((RUNS, RUN, PAD), bf16)),
        in_specs=[pl.BlockSpec(memory_space=pltpu.SMEM)] * 2 + [pl.BlockSpec(memory_space=pltpu.HBM)] * 3,
        out_specs=(pl.BlockSpec(memory_space=pltpu.HBM),) * 3,
        scratch_shapes=[
            pltpu.SMEM((RUNS,), jnp.int32),
            V((TOKENS, PAD), bf16), V((KVW, TOKENS), f32),
            V((TOKENS, ROWS), f32), V((TOKENS, ROWS), f32), V((TOKENS // SMALL * 8, ROWS), f32),
            V((ROWS, PAD), bf16), V((PAD, ROWS), bf16), V((ROWS, LAT), bf16), V((LAT, ROWS), bf16),
            V((2 * RUN, HEADS * KVW), bf16), V((2 * RUN, HEADS * LAT), bf16), V((2, TOKENS, ROWS), bf16),
            pltpu.SemaphoreType.DMA((TOKENS // BIG,)), pltpu.SemaphoreType.DMA((2, CHUNKS)), pltpu.SemaphoreType.DMA((2,)), pltpu.SemaphoreType.DMA((2,)),
        ],
        compiler_params=pltpu.CompilerParams(vmem_limit_bytes=62 * 2**20),
        cost_estimate=pl.CostEstimate(flops=46 * 10**9, bytes_accessed=2 * 10**7, transcendentals=10**7),
        name="attend",
    )(positions, runs, query, out_grad, gathered)


def settle_kernel(qg_in, lg_in, qg_ref, lg_ref, sem):
    copies = [pltpu.make_async_copy(qg_in.at[pl.ds(i * 32, 32)], qg_ref.at[pl.ds(i * 32, 32)], sem.at[i]) for i in range(4)]
    copies.append(pltpu.make_async_copy(lg_in, lg_ref, sem.at[4]))
    for c in copies:
        c.start()
    for c in copies:
        c.wait()


def settle(query_grad, latent_grad):
    return pl.pallas_call(
        settle_kernel,
        out_shape=(jax.ShapeDtypeStruct(query_grad.shape, query_grad.dtype), jax.ShapeDtypeStruct(latent_grad.shape, latent_grad.dtype)),
        in_specs=[pl.BlockSpec(memory_space=pltpu.HBM), pl.BlockSpec(memory_space=pl.ANY)],
        out_specs=(pl.BlockSpec(memory_space=pltpu.HBM),) * 2,
        scratch_shapes=[pltpu.SemaphoreType.DMA((5,))],
        cost_estimate=pl.CostEstimate(flops=0, bytes_accessed=5 * 10**6, transcendentals=0),
        name="settle",
    )(query_grad, latent_grad)


def per_device(query, latent, out_grad, positions):
    gathered, runs = gather(positions, latent)
    ds, keys, part = attend(positions, runs, query, out_grad, gathered.reshape(RUNS, RUN, PAD))
    latent_grad, query_grad = scatter(part.reshape(4, 4, 4, RUN, PAD), ds, keys)
    return settle(query_grad, latent_grad)


def solution(mesh):
    return jax.shard_map(
        per_device,
        mesh=mesh,
        in_specs=(P("seq", "tp"), P(("seq", "tp"), None), P("seq", "tp"), P("seq")),
        out_specs=(P("seq", "tp"), P(("seq", "tp"), None)),
        check_vma=False,
    )
```

```python
import math

import jax, jax.numpy as jnp
from jax import lax
from jax.experimental import pallas as pl
from jax.experimental.pallas import tpu as pltpu
from jax.sharding import PartitionSpec as P

LAT=512; KVW=576; PAD=640
SCALE = 192.0 ** -0.5
TO_BASE_2 = SCALE * math.log2(math.e)
MASKED = -1e30
TOKENS = 4096
RUN = 64
RUNS = TOKENS // RUN
HEADS = 16
GROUP = 8
ROWS = GROUP * RUN
HUGE, BIG, SMALL = 2048, 1024, 512
CHUNKS = 2 * HEADS // GROUP
QUARTERS = TOKENS // BIG
PIECE = 2048
PIECES = TOKENS // PIECE
SLICES = CHUNKS * PIECES
PLAN = (0, 1, 2, 2, 0, 1)
MESH = pl.DeviceIdType.MESH
PARTS = (((0, 1, 2), 0, 256), ((1, 2, 0), 256, 256), ((2, 0, 1), 512, 128))
SUM_PARTS = (((0, 2, 1), 0, 256), ((1, 2, 0), 256, 256), ((2, 1, 0), 512, 128))


def coords():
    seq, tp = lax.axis_index("seq"), lax.axis_index("tp")
    x = lax.rem(seq, 4)
    z = lax.rem(seq // 4, 2) * 2 + tp // 2
    y = seq // 8
    return [x, y, z], lax.rem(tp, 2)


def device(place, core):
    x, y, z = place
    return ((y * 2 + z // 2) * 4 + x, lax.rem(z, 2) * 2 + core)


def moved(place, axis, by):
    out = list(place)
    out[axis] = lax.rem(place[axis] + by, 4)
    return out


def greet(place, core, opposite=False):
    barrier = pltpu.get_barrier_semaphore()
    steps = (1, 2, 3) if opposite else (1, 3)
    for axis in range(3):
        for by in steps:
            pl.semaphore_signal(barrier, inc=1, device_id=device(moved(place, axis, by), core), device_id_type=MESH)
    pl.semaphore_signal(barrier, inc=1, device_id=device(place, 1 - core), device_id_type=MESH)
    pl.semaphore_wait(barrier, 3 * len(steps) + 1)


def gather_kernel(pos_ref, lat_ref, out_ref, runs_ref, own, tags, tags_f, sem, send, recv):
    place, core = coords()
    run = pos_ref[lax.rem(place[2], 2) * 64] // 64
    own[:, :KVW] = lat_ref[...]
    own[:, KVW:] = jnp.full((32, PAD - KVW), run.astype(jnp.float32)).astype(jnp.bfloat16)
    put = pltpu.make_async_copy(own, out_ref.at[place[0], place[1], place[2], core], sem)
    put.start()
    greet(place, core, True)
    put.wait()
    sent = []

    def copy(ref, dev):
        i = len(sent)
        c = pltpu.make_async_remote_copy(ref, ref, send.at[i], recv.at[i], device_id=dev, device_id_type=MESH)
        c.start()
        sent.append(c)
        return c

    def shards(order, lane, width, at1, at2, at3, rows=(0, 32)):
        at = [None] * 3
        for axis, v in zip(order, (at1, at2, at3)):
            at[axis] = pl.ds(0, 4) if v is None else lax.rem(place[axis] + v, 4)
        return out_ref.at[at[0], at[1], at[2], core, pl.ds(*rows), pl.ds(lane, width)]

    sibling = device(place, 1 - core)
    twins = []
    one, two, three = {}, {}, {}
    steps = (1, 3, 2)

    def spread(p, d1):
        order, lane, width = PARTS[p]
        for by in steps:
            two[p, d1, by] = copy(shards(order, lane, width, d1, 0, 0), device(moved(place, order[1], by), core))

    def shift(p, d2):
        order, lane, width = PARTS[p]
        for by in (1, 3):
            three[p, d2, by] = copy(shards(order, lane, width, None, d2, 0), device(moved(place, order[2], by), core))

    def forward(p, d2):
        order, lane, width = PARTS[p]
        three[p, d2, 1].wait_recv()
        three[p, d2, 4] = copy(shards(order, lane, width, None, d2, 3, (0, 16)), device(moved(place, order[2], 1), core))
        three[p, d2, 3].wait_recv()
        three[p, d2, 5] = copy(shards(order, lane, width, None, d2, 1, (16, 16)), device(moved(place, order[2], 3), core))

    def arrive(p, d2):
        for d1 in (0, 1, 3, 2):
            two[p, d1, {3: 1, 1: 3, 2: 2}[d2]].wait_recv()

    n = range(len(PARTS))
    for p in n:
        order, lane, width = PARTS[p]
        for by in steps:
            one[p, by] = copy(shards(order, lane, width, 0, 0, 0), device(moved(place, order[0], by), core))
    for p in n:
        spread(p, 0)
    for by in steps:
        for p in n:
            one[p, by].wait_recv()
            spread(p, {1: 3, 3: 1, 2: 2}[by])
    for p in n:
        shift(p, 0)
    for d2 in (3, 1, 2):
        for p in n:
            arrive(p, d2)
            shift(p, d2)
    for p in n:
        order, lane, width = PARTS[p]
        twins.append(copy(shards(order, lane, width, None, None, 0), sibling))
    for d2 in (0, 3, 1, 2):
        for p in n:
            forward(p, d2)
    for p in n:
        order, lane, width = PARTS[p]
        twins.append(copy(shards(order, lane, width, None, None, 3), sibling))
        twins.append(copy(shards(order, lane, width, None, None, 1), sibling))
    for p in (2, 0, 1):
        order, lane, width = PARTS[p]
        for d2 in (0, 3, 1, 2):
            three[p, d2, 4].wait_recv()
            three[p, d2, 5].wait_recv()
            twins.append(copy(shards(order, lane, width, None, d2, 2), sibling))
        if p == 2:
            load_tags = pltpu.make_async_copy(out_ref.at[:, :, :, core, pl.ds(0, 16), pl.ds(LAT, 128)], tags, sem)
            load_tags.start()
    load_tags.wait()
    tags_f[...] = jnp.zeros_like(tags_f)
    tags_f[:RUNS, :] = tags[:, :, :, 0, :].reshape(RUNS, 128).astype(jnp.float32)
    runs_ref[...] = tags_f[...].T[KVW - LAT:KVW - LAT + 8, :].astype(jnp.int32)
    for t in twins:
        t.wait_recv()
    for s in sent:
        s.wait_send()


N_GATHER = 3 * (3 + 12 + 8 + 1 + 8 + 2 + 4)


def gather(positions, latent):
    return pl.pallas_call(
        gather_kernel,
        out_shape=(jax.ShapeDtypeStruct((4, 4, 4, 2, 32, PAD), jnp.bfloat16), jax.ShapeDtypeStruct((8, 128), jnp.int32)),
        in_specs=[pl.BlockSpec(memory_space=pltpu.SMEM), pl.BlockSpec(memory_space=pltpu.VMEM)],
        out_specs=(pl.BlockSpec(memory_space=pltpu.HBM), pl.BlockSpec(memory_space=pltpu.VMEM)),
        scratch_shapes=[
            pltpu.VMEM((32, PAD), jnp.bfloat16),
            pltpu.VMEM((4, 4, 4, 16, 128), jnp.bfloat16),
            pltpu.VMEM((128, 128), jnp.float32),
            pltpu.SemaphoreType.DMA,
            pltpu.SemaphoreType.DMA((N_GATHER,)),
            pltpu.SemaphoreType.DMA((N_GATHER,)),
        ],
        compiler_params=pltpu.CompilerParams(collective_id=0, has_side_effects=True),
        cost_estimate=pl.CostEstimate(flops=0, bytes_accessed=10 * 2**20, transcendentals=0),
        name="gather_latent",
    )(positions, latent)


def dropped(axis, done):
    return axis - sum(1 for a in done if a < axis)


def at(ref, dim, value, rows=None):
    index = [slice(None)] * dim + [value]
    view = ref.at[tuple(index)]
    if rows is not None:
        lead = len(view.shape) - 2
        view = view.at[tuple([slice(None)] * lead + [pl.ds(*rows)])]
    return view


def scatter_kernel(part_ref, ds_ref, keys_ref, out_ref, qg_ref, mine, theirs, keep, wire, relay, landed,
                   keys, keys_t, ds_in, qg_t, qg_out, sem, kt_sem, ds_sem, qg_sem, send, recv):
    place, core = coords()
    load_keys = pltpu.make_async_copy(keys_ref, keys, kt_sem)
    load_keys.start()

    def load_ds(i):
        return pltpu.make_async_copy(ds_ref.at[i // PIECES, pl.ds(lax.rem(i, PIECES) * PIECE, PIECE)], ds_in.at[lax.rem(i, 2)], ds_sem.at[lax.rem(i, 2)])

    load_ds(0).start()

    def slice_of_work(i, _):
        @pl.when(i + 1 < SLICES)
        def _():
            load_ds(i + 1).start()
        load_ds(i).wait()
        c, k = i // PIECES, lax.rem(i, PIECES)

        @pl.when(k == 0)
        def _():
            qg_t[...] = jnp.zeros_like(qg_t)
        qg_t[...] += jnp.dot(keys_t[:, pl.ds(pl.multiple_of(k * PIECE, PIECE), PIECE)], ds_in[lax.rem(i, 2)], preferred_element_type=jnp.float32)

        @pl.when(k == PIECES - 1)
        def _():
            row = pl.multiple_of((c // 2) * RUN, RUN)
            for h in range(0, GROUP, 2):
                a = qg_t[:, h * RUN:h * RUN + 2 * RUN].T.astype(jnp.bfloat16)
                lane = pl.multiple_of(lax.rem(c, 2) * (GROUP * KVW) + h * KVW, 128)
                qg_out[pl.ds(row, RUN), pl.ds(lane, 2 * KVW)] = jnp.concatenate([a[:RUN], a[RUN:]], axis=1)
        return 0

    done_work = [0]

    def work(n):
        first = done_work[0]
        done_work[0] += n
        lax.fori_loop(first, first + n, slice_of_work, 0)

    greet(place, core, True)
    count = [0]
    sent = []

    def copy(src, dst, dev):
        i = count[0]
        count[0] += 1
        c = pltpu.make_async_remote_copy(src, dst, send.at[i], recv.at[i], device_id=dev, device_id_type=MESH)
        c.start()
        sent.append(c)
        return c

    sibling = device(place, 1 - core)
    swaps, loads = [], []
    for n, (order, lane, width) in enumerate(SUM_PARTS):
        other = part_ref.at[:, :, :, pl.ds(32 * (1 - core), 32), pl.ds(lane, width)]
        swaps.append(copy(other, theirs[n], sibling))
        load = pltpu.make_async_copy(part_ref.at[:, :, :, pl.ds(32 * core, 32), pl.ds(lane, width)], mine[n], sem.at[n])
        load.start()
        loads.append(load)

    load_keys.wait()

    def turn(j, _):
        o = pl.multiple_of(j * 256, 256)
        keys_t[:, pl.ds(o, 256)] = keys[pl.ds(o, 256), :KVW].T
        return 0

    lax.fori_loop(0, TOKENS // 256, turn, 0)
    work(PLAN[0])
    halves = ((0, 16), (16, 16))

    def parts(phase):
        for n, (order, lane, width) in enumerate(SUM_PARTS):
            axis = order[phase]
            yield n, axis, dropped(axis, order[:phase]), place[axis], lane, width

    started = []
    for n, axis, dim, me, lane, width in parts(0):
        k, w, rl, ld = keep[n][0], wire[n][0], relay[n], landed[n][0]
        right, left, opp = (lax.rem(me + i, 4) for i in (1, 3, 2))
        rdev, ldev = device(moved(place, axis, 1), core), device(moved(place, axis, 3), core)
        loads[n].wait()
        swaps[n].wait_recv()

        def fill(v):
            at(k, dim, v)[...] = at(mine[n], dim, v)[...].astype(jnp.float32) + at(theirs[n], dim, v)[...].astype(jnp.float32)

        fill(opp)
        at(w, dim, opp)[...] = at(k, dim, opp)[...].astype(w.dtype)
        c0 = copy(at(w, dim, opp, halves[0]), rl.at[0], rdev)
        c1 = copy(at(w, dim, opp, halves[1]), rl.at[1], ldev)
        fill(right)
        at(w, dim, right, halves[1])[...] = at(k, dim, right, halves[1])[...].astype(w.dtype)
        c2 = copy(at(w, dim, right, halves[1]), ld.at[0, 1], rdev)
        fill(left)
        at(w, dim, left, halves[0])[...] = at(k, dim, left, halves[0])[...].astype(w.dtype)
        c3 = copy(at(w, dim, left, halves[0]), ld.at[1, 0], ldev)
        fill(me)
        started.append((c0, c1, c2, c3))
        work(PLAN[1])
    ended = []
    for n, axis, dim, me, lane, width in parts(0):
        k, w, rl, ld = keep[n][0], wire[n][0], relay[n], landed[n][0]
        right, left = lax.rem(me + 1, 4), lax.rem(me + 3, 4)
        rdev, ldev = device(moved(place, axis, 1), core), device(moved(place, axis, 3), core)
        c0, c1, c2, c3 = started[n]
        c0.wait_recv()
        at(w, dim, right, halves[0])[...] = (at(k, dim, right, halves[0])[...] + rl[0].astype(jnp.float32)).astype(w.dtype)
        c4 = copy(at(w, dim, right, halves[0]), ld.at[0, 0], rdev)
        c1.wait_recv()
        at(w, dim, left, halves[1])[...] = (at(k, dim, left, halves[1])[...] + rl[1].astype(jnp.float32)).astype(w.dtype)
        c5 = copy(at(w, dim, left, halves[1]), ld.at[1, 1], ldev)
        ended.append((c2, c3, c4, c5))
    work(PLAN[2])
    going = []
    for phase in (1, 2):
        for n, axis, dim, me, lane, width in parts(phase):
            if phase == 1:
                for c in ended[n]:
                    c.wait_recv()
                ld = landed[n][0]
                was = list(parts(0))[n]
                for h in (0, 1):
                    keep[n][1].at[:, :, pl.ds(*halves[h])][...] = (at(keep[n][0], was[2], was[3], halves[h])[...] + ld[0, h].astype(jnp.float32)) + ld[1, h].astype(jnp.float32)
            else:
                for c in going[n]:
                    c.wait_recv()
                ld = landed[n][1]
                was = list(parts(1))[n]
                keep[n][2][...] = (at(keep[n][1], was[2], was[3])[...] + ld[0].astype(jnp.float32)) + (ld[1].astype(jnp.float32) + ld[2].astype(jnp.float32))
            k, w, ld = keep[n][phase], wire[n][phase], landed[n][phase]
            sends = []
            for slot, by in enumerate((2, 1, 3)):
                v = lax.rem(me + by, 4)
                at(w, dim, v)[...] = at(k, dim, v)[...].astype(w.dtype)
                sends.append(copy(at(w, dim, v), ld.at[slot], device(moved(place, axis, by), core)))
            if phase == 1:
                going.append(sends)
            else:
                going[n] = sends
        work(PLAN[1 + 2 * phase])
        if phase == 2:
            put = pltpu.make_async_copy(qg_out, qg_ref, qg_sem)
            put.start()
    for n, axis, dim, me, lane, width in parts(2):
        for c in going[n]:
            c.wait_recv()
        ld = landed[n][2]
        total = (at(keep[n][2], 0, me)[...] + ld[0]) + (ld[1] + ld[2])
        real = min(width, KVW - lane)
        out_ref[:, pl.ds(lane, real)] = total[:, :real]
    put.wait()
    for s in sent:
        s.wait_send()


N_SCATTER = 3 + 3 * (6 + 3 + 3)
WIRES = (jnp.bfloat16, jnp.bfloat16, jnp.float32)


def scatter(part, ds, keys):
    V, f32, bf16 = pltpu.VMEM, jnp.float32, jnp.bfloat16
    mine = [V((4, 4, 4, 32, w), bf16) for _, _, w in PARTS]
    keep = [[V((4,) * (3 - p) + (32, w), f32) for p in range(3)] for _, _, w in PARTS]
    wire = [[V((4,) * (3 - p) + (32, w), WIRES[p]) for p in range(3)] for _, _, w in PARTS]
    relay = [V((2, 4, 4, 16, w), WIRES[0]) for _, _, w in PARTS]
    landed = [[V((2, 2, 4, 4, 16, w), WIRES[0]), V((3, 4, 32, w), WIRES[1]), V((3, 32, w), WIRES[2])] for _, _, w in PARTS]
    return pl.pallas_call(
        scatter_kernel,
        out_shape=(jax.ShapeDtypeStruct((32, KVW), f32), jax.ShapeDtypeStruct((2 * RUN, HEADS * KVW), bf16)),
        in_specs=[pl.BlockSpec(memory_space=pltpu.HBM)] * 3,
        out_specs=(pl.BlockSpec(memory_space=pltpu.VMEM), pl.BlockSpec(memory_space=pltpu.HBM)),
        scratch_shapes=[
            mine, list(mine), keep, wire, relay, landed,
            V((TOKENS, PAD), bf16), V((KVW, TOKENS), bf16), V((2, PIECE, ROWS), bf16), V((KVW, ROWS), f32), V((2 * RUN, HEADS * KVW), bf16),
            pltpu.SemaphoreType.DMA((3,)), pltpu.SemaphoreType.DMA, pltpu.SemaphoreType.DMA((2,)), pltpu.SemaphoreType.DMA,
            pltpu.SemaphoreType.DMA((N_SCATTER,)),
            pltpu.SemaphoreType.DMA((N_SCATTER,)),
        ],
        compiler_params=pltpu.CompilerParams(collective_id=1, has_side_effects=True, vmem_limit_bytes=56 * 2**20),
        cost_estimate=pl.CostEstimate(flops=10**10, bytes_accessed=3 * 10**7, transcendentals=0),
        name="scatter_latent_grad",
    )(part, ds, keys)


def attend_kernel(pos_ref, runs_ref, q_ref, do_ref, kg_ref, ds_ref, keys_ref, part_ref,
                  chip_of, keys, acc, exps, gws, tops, qs, qs_t, dos, dos_t, q_in, do_in, ds_out,
                  key_sem, in_sem, out_sem, ds_sem):
    f32, bf16 = jnp.float32, jnp.bfloat16
    copy_keys = pltpu.make_async_copy(keys, keys_ref, out_sem.at[1])

    def inputs(c):
        row = pl.ds(pl.multiple_of((c // 2) * RUN, RUN), RUN)
        out = []
        for i, (ref, to, width) in enumerate(((q_ref, q_in, GROUP * KVW), (do_ref, do_in, GROUP * LAT))):
            lane = pl.ds(pl.multiple_of(lax.rem(c, 2) * width, 128), width)
            out.append(pltpu.make_async_copy(ref.at[row, lane], to.at[row, lane], in_sem.at[i, c]))
        return out

    def take(c, _):
        for copy in inputs(c):
            copy.start()
        return 0

    take(0, 0)

    def place(chip, _):
        chip_of[runs_ref[0, chip]] = chip
        return 0

    lax.fori_loop(0, RUNS, place, 0)

    def fetch(j, _):
        pltpu.make_async_copy(kg_ref.at[chip_of[j]], keys.at[pl.ds(j * RUN, RUN)], key_sem.at[j // (BIG // RUN)]).start()
        return 0

    lax.fori_loop(0, BIG // RUN, fetch, 0)
    lax.fori_loop(BIG // RUN, RUNS, fetch, 0)
    lax.fori_loop(1, CHUNKS, take, 0)

    def await_keys(t, _):
        tile = keys.at[pl.ds(pl.multiple_of(t * BIG, BIG), BIG)]
        pltpu.make_async_copy(tile, tile, key_sem.at[t]).wait()
        return 0

    acc[...] = jnp.zeros_like(acc)
    qs[:, LAT:] = jnp.zeros((ROWS, PAD - LAT), bf16)

    def chunk(c, _):
        for copy in inputs(c):
            copy.wait()
        half, block, slot = lax.rem(c, 2), c // 2, lax.rem(c, 2)
        run = pos_ref[block * RUN] // RUN
        row = pl.multiple_of(block * RUN, RUN)
        for h in range(0, GROUP, 2):
            v = q_in[pl.ds(row, RUN), pl.ds(pl.multiple_of(half * (GROUP * KVW) + h * KVW, 128), 2 * KVW)]
            qs[h * RUN:h * RUN + RUN, :KVW] = v[:, :KVW]
            qs[h * RUN + RUN:h * RUN + 2 * RUN, :KVW] = v[:, KVW:]
            d = do_in[pl.ds(row, RUN), pl.ds(pl.multiple_of(half * (GROUP * LAT) + h * LAT, 128), 2 * LAT)]
            dos[h * RUN:h * RUN + RUN, :] = d[:, :LAT]
            dos[h * RUN + RUN:h * RUN + 2 * RUN, :] = d[:, LAT:]
        qs_t[...] = qs[...].T
        dos_t[...] = dos[...].T
        full = run // (SMALL // RUN)
        huge = full // 4
        rest = lax.rem(full, 4)
        big = rest // 2
        odd = lax.rem(rest, 2) == 1
        last = huge * 4 + big * 2

        def scan(u, size, masked, carry):
            m, l, d = carry

            @pl.when(c == 0)
            def _():
                for i in range(max(size // BIG, 1)):
                    await_keys(u // 2 + i, 0)
            o = pl.multiple_of(u * SMALL, SMALL)
            tile = keys[pl.ds(o, size), :]
            s = jnp.dot(tile, qs_t[...], preferred_element_type=f32)
            g = jnp.dot(tile[:, :LAT], dos_t[...], preferred_element_type=f32)
            if masked:
                key = lax.broadcasted_iota(jnp.int32, (size, ROWS), 0)
                tok = lax.broadcasted_iota(jnp.int32, (size, ROWS), 1) % RUN
                s = jnp.where(key - tok <= run * RUN - o, s, MASKED)
            s = s * TO_BASE_2
            top = jnp.maximum(m, jnp.max(s, axis=0, keepdims=True))
            e = jnp.exp2(s - top)
            exps[pl.ds(o, size), :] = e
            gws[pl.ds(o, size), :] = g
            tops[pl.ds(pl.multiple_of(u * 8, 8), 8), :] = jnp.broadcast_to(top, (8, ROWS))
            a = jnp.exp2(m - top)
            return top, l * a + jnp.sum(e, axis=0, keepdims=True), d * a + jnp.sum(e * g, axis=0, keepdims=True)

        start = (jnp.full((1, ROWS), MASKED, f32), jnp.zeros((1, ROWS), f32), jnp.zeros((1, ROWS), f32))
        carry = lax.fori_loop(0, huge, lambda t, s: scan(t * 4, HUGE, False, s), start)
        carry = lax.fori_loop(0, big, lambda t, s: scan(huge * 4, BIG, False, s), carry)
        m, l, d = lax.cond(odd, lambda: scan(last, BIG, True, carry), lambda: scan(last, SMALL, True, carry))

        @pl.when(c == 0)
        def _():
            lax.fori_loop(last // 2 + 1, TOKENS // BIG, await_keys, 0)
            copy_keys.start()
        share = 1.0 / l
        delta = d * share

        @pl.when(c >= 2)
        def _():
            pltpu.make_async_copy(ds_out.at[slot], ds_ref.at[c], ds_sem.at[slot]).wait()

        def leave_ds(k, _):
            span = pl.ds(pl.multiple_of(k * BIG, BIG), BIG)
            pltpu.make_async_copy(ds_out.at[slot, span], ds_ref.at[c, span], ds_sem.at[slot]).start()
            return 0

        def back(u, size):
            o = pl.multiple_of(u * SMALL, SMALL)
            span = pl.ds(o, size)
            w = exps[span, :] * (jnp.exp2(tops[pl.ds(pl.multiple_of(u * 8, 8), 8), :][:1] - m) * share)
            ds = (w * ((gws[span, :] - delta) * SCALE)).astype(bf16)
            ds_out[slot, span, :] = ds
            nt = (((1,), (1,)), ((), ()))
            acc[:, span] += lax.dot_general(qs_t[:KVW], ds, nt, preferred_element_type=f32)
            acc[:LAT, span] += lax.dot_general(dos_t[...], w.astype(bf16), nt, preferred_element_type=f32)
            for k in range(max(size // BIG, 1)):
                leave_ds(u // 2 + k, 0)
            return 0

        def blank(u, _):
            ds_out[slot, pl.ds(pl.multiple_of(u * SMALL, SMALL), SMALL), :] = jnp.zeros((SMALL, ROWS), bf16)
            return 0

        lax.fori_loop(full + 1, TOKENS // SMALL, blank, 0)
        lax.fori_loop(last // 2 + 1, QUARTERS, leave_ds, 0)
        lax.fori_loop(0, huge, lambda t, _: back(t * 4, HUGE), 0)
        lax.fori_loop(0, big, lambda t, _: back(huge * 4, BIG), 0)

        @pl.when(odd)
        def _():
            back(last, BIG)

        @pl.when(jnp.logical_not(odd))
        def _():
            back(last, SMALL)

        return 0

    lax.fori_loop(0, CHUNKS, chunk, 0)
    copy_keys.wait()

    def leave(j, _):
        o = pl.multiple_of(j * 256, 256)
        keys[pl.ds(o, 256), :KVW] = acc[:, pl.ds(o, 256)].astype(bf16).T
        for i in range(4):
            pltpu.make_async_copy(keys.at[pl.ds(o + i * RUN, RUN)], part_ref.at[chip_of[j * 4 + i]], out_sem.at[0]).start()
        return 0

    lax.fori_loop(0, TOKENS // 256, leave, 0)
    for slot in range(2):
        pltpu.make_async_copy(ds_out.at[slot], ds_ref.at[0], ds_sem.at[slot]).wait()
    pltpu.make_async_copy(keys, keys, out_sem.at[0]).wait()


def attend(positions, runs, query, out_grad, gathered):
    V, f32, bf16 = pltpu.VMEM, jnp.float32, jnp.bfloat16
    return pl.pallas_call(
        attend_kernel,
        out_shape=(jax.ShapeDtypeStruct((CHUNKS, TOKENS, ROWS), bf16), jax.ShapeDtypeStruct((TOKENS, PAD), bf16),
                   jax.ShapeDtypeStruct((RUNS, RUN, PAD), bf16)),
        in_specs=[pl.BlockSpec(memory_space=pltpu.SMEM)] * 2 + [pl.BlockSpec(memory_space=pltpu.HBM)] * 3,
        out_specs=(pl.BlockSpec(memory_space=pltpu.HBM),) * 3,
        scratch_shapes=[
            pltpu.SMEM((RUNS,), jnp.int32),
            V((TOKENS, PAD), bf16), V((KVW, TOKENS), f32),
            V((TOKENS, ROWS), f32), V((TOKENS, ROWS), f32), V((TOKENS // SMALL * 8, ROWS), f32),
            V((ROWS, PAD), bf16), V((PAD, ROWS), bf16), V((ROWS, LAT), bf16), V((LAT, ROWS), bf16),
            V((2 * RUN, HEADS * KVW), bf16), V((2 * RUN, HEADS * LAT), bf16), V((2, TOKENS, ROWS), bf16),
            pltpu.SemaphoreType.DMA((TOKENS // BIG,)), pltpu.SemaphoreType.DMA((2, CHUNKS)), pltpu.SemaphoreType.DMA((2,)), pltpu.SemaphoreType.DMA((2,)),
        ],
        compiler_params=pltpu.CompilerParams(vmem_limit_bytes=62 * 2**20),
        cost_estimate=pl.CostEstimate(flops=46 * 10**9, bytes_accessed=2 * 10**7, transcendentals=10**7),
        name="attend",
    )(positions, runs, query, out_grad, gathered)


def settle_kernel(qg_in, lg_in, qg_ref, lg_ref, qg_buf, lg_buf, sem):
    pieces = [(qg_in.at[pl.ds(i * 32, 32)], qg_buf.at[pl.ds(i * 32, 32)], qg_ref.at[pl.ds(i * 32, 32)]) for i in range(4)]
    pieces.append((lg_in, lg_buf, lg_ref))
    loads = [pltpu.make_async_copy(a, b, sem.at[0, i]) for i, (a, b, _) in enumerate(pieces)]
    stores = [pltpu.make_async_copy(b, c, sem.at[1, i]) for i, (_, b, c) in enumerate(pieces)]
    for load in loads:
        load.start()
    for load, store in zip(loads, stores):
        load.wait()
        store.start()
    for store in stores:
        store.wait()


def settle(query_grad, latent_grad):
    return pl.pallas_call(
        settle_kernel,
        out_shape=(jax.ShapeDtypeStruct(query_grad.shape, query_grad.dtype), jax.ShapeDtypeStruct(latent_grad.shape, latent_grad.dtype)),
        in_specs=[pl.BlockSpec(memory_space=pltpu.HBM), pl.BlockSpec(memory_space=pl.ANY)],
        out_specs=(pl.BlockSpec(memory_space=pltpu.HBM),) * 2,
        scratch_shapes=[pltpu.VMEM(query_grad.shape, query_grad.dtype), pltpu.VMEM(latent_grad.shape, latent_grad.dtype), pltpu.SemaphoreType.DMA((2, 5))],
        cost_estimate=pl.CostEstimate(flops=0, bytes_accessed=5 * 10**6, transcendentals=0),
        name="settle",
    )(query_grad, latent_grad)


def per_device(query, latent, out_grad, positions):
    gathered, runs = gather(positions, latent)
    ds, keys, part = attend(positions, runs, query, out_grad, gathered.reshape(RUNS, RUN, PAD))
    latent_grad, query_grad = scatter(part.reshape(4, 4, 4, RUN, PAD), ds, keys)
    return settle(query_grad, latent_grad)


def solution(mesh):
    return jax.shard_map(
        per_device,
        mesh=mesh,
        in_specs=(P("seq", "tp"), P(("seq", "tp"), None), P("seq", "tp"), P("seq")),
        out_specs=(P("seq", "tp"), P(("seq", "tp"), None)),
        check_vma=False,
    )
```

```python
import math

import jax, jax.numpy as jnp
from jax import lax
from jax.experimental import pallas as pl
from jax.experimental.pallas import tpu as pltpu
from jax.sharding import PartitionSpec as P

LAT=512; KVW=576; PAD=640
SCALE = 192.0 ** -0.5
TO_BASE_2 = SCALE * math.log2(math.e)
MASKED = -1e30
TOKENS = 4096
RUN = 64
RUNS = TOKENS // RUN
HEADS = 16
GROUP = 8
ROWS = GROUP * RUN
HUGE, BIG, SMALL = 2048, 1024, 256
CHUNKS = 2 * HEADS // GROUP
QUARTERS = TOKENS // BIG
PIECE = 2048
PIECES = TOKENS // PIECE
SLICES = CHUNKS * PIECES
PLAN = (0, 1, 2, 2, 0, 1)
MESH = pl.DeviceIdType.MESH
PARTS = (((0, 1, 2), 0, 256), ((1, 2, 0), 256, 256), ((2, 0, 1), 512, 128))
SUM_PARTS = (((0, 2, 1), 0, 256), ((1, 2, 0), 256, 256), ((2, 1, 0), 512, 128))


def coords():
    seq, tp = lax.axis_index("seq"), lax.axis_index("tp")
    x = lax.rem(seq, 4)
    z = lax.rem(seq // 4, 2) * 2 + tp // 2
    y = seq // 8
    return [x, y, z], lax.rem(tp, 2)


def device(place, core):
    x, y, z = place
    return ((y * 2 + z // 2) * 4 + x, lax.rem(z, 2) * 2 + core)


def moved(place, axis, by):
    out = list(place)
    out[axis] = lax.rem(place[axis] + by, 4)
    return out


def greet(place, core, opposite=False):
    barrier = pltpu.get_barrier_semaphore()
    steps = (1, 2, 3) if opposite else (1, 3)
    for axis in range(3):
        for by in steps:
            pl.semaphore_signal(barrier, inc=1, device_id=device(moved(place, axis, by), core), device_id_type=MESH)
    pl.semaphore_signal(barrier, inc=1, device_id=device(place, 1 - core), device_id_type=MESH)
    pl.semaphore_wait(barrier, 3 * len(steps) + 1)


def gather_kernel(pos_ref, lat_ref, out_ref, runs_ref, own, tags, tags_f, sem, send, recv):
    place, core = coords()
    run = pos_ref[lax.rem(place[2], 2) * 64] // 64
    own[:, :KVW] = lat_ref[...]
    own[:, KVW:] = jnp.full((32, PAD - KVW), run.astype(jnp.float32)).astype(jnp.bfloat16)
    put = pltpu.make_async_copy(own, out_ref.at[place[0], place[1], place[2], core], sem)
    put.start()
    greet(place, core, True)
    sent = []

    def copy(ref, dev, source=None):
        i = len(sent)
        c = pltpu.make_async_remote_copy(ref if source is None else source, ref, send.at[i], recv.at[i], device_id=dev, device_id_type=MESH)
        c.start()
        sent.append(c)
        return c

    def shards(order, lane, width, at1, at2, at3, rows=(0, 32)):
        at = [None] * 3
        for axis, v in zip(order, (at1, at2, at3)):
            at[axis] = pl.ds(0, 4) if v is None else lax.rem(place[axis] + v, 4)
        return out_ref.at[at[0], at[1], at[2], core, pl.ds(*rows), pl.ds(lane, width)]

    sibling = device(place, 1 - core)
    twins = []
    one, two, three = {}, {}, {}
    steps = (1, 3, 2)

    def spread(p, d1):
        order, lane, width = PARTS[p]
        for by in steps:
            two[p, d1, by] = copy(shards(order, lane, width, d1, 0, 0), device(moved(place, order[1], by), core), None if d1 else own.at[:, pl.ds(lane, width)])

    def shift(p, d2):
        order, lane, width = PARTS[p]
        for by in (1, 3):
            three[p, d2, by] = copy(shards(order, lane, width, None, d2, 0), device(moved(place, order[2], by), core))

    def forward(p, d2):
        order, lane, width = PARTS[p]
        three[p, d2, 1].wait_recv()
        three[p, d2, 4] = copy(shards(order, lane, width, None, d2, 3, (0, 16)), device(moved(place, order[2], 1), core))
        three[p, d2, 3].wait_recv()
        three[p, d2, 5] = copy(shards(order, lane, width, None, d2, 1, (16, 16)), device(moved(place, order[2], 3), core))

    def arrive(p, d2):
        for d1 in (0, 1, 3, 2):
            two[p, d1, {3: 1, 1: 3, 2: 2}[d2]].wait_recv()

    n = range(len(PARTS))
    for p in n:
        order, lane, width = PARTS[p]
        for by in steps:
            one[p, by] = copy(shards(order, lane, width, 0, 0, 0), device(moved(place, order[0], by), core), own.at[:, pl.ds(lane, width)])
    for p in n:
        spread(p, 0)
    for by in steps:
        for p in n:
            one[p, by].wait_recv()
            spread(p, {1: 3, 3: 1, 2: 2}[by])
    put.wait()
    for p in n:
        shift(p, 0)
    for d2 in (3, 1, 2):
        for p in n:
            arrive(p, d2)
            shift(p, d2)
    for p in n:
        order, lane, width = PARTS[p]
        twins.append(copy(shards(order, lane, width, None, None, 0), sibling))
    for d2 in (0, 3, 1, 2):
        for p in n:
            forward(p, d2)
    for p in n:
        order, lane, width = PARTS[p]
        twins.append(copy(shards(order, lane, width, None, None, 3), sibling))
        twins.append(copy(shards(order, lane, width, None, None, 1), sibling))
    tagged = [p for p in n if PARTS[p][1] == LAT][0]
    for p in (tagged, *[p for p in n if p != tagged]):
        order, lane, width = PARTS[p]
        for d2 in (0, 3, 1, 2):
            three[p, d2, 4].wait_recv()
            three[p, d2, 5].wait_recv()
            twins.append(copy(shards(order, lane, width, None, d2, 2), sibling))
        if p == tagged:
            load_tags = pltpu.make_async_copy(out_ref.at[:, :, :, core, pl.ds(0, 16), pl.ds(LAT, 128)], tags, sem)
            load_tags.start()
    load_tags.wait()
    tags_f[...] = jnp.zeros_like(tags_f)
    tags_f[:RUNS, :] = tags[:, :, :, 0, :].reshape(RUNS, 128).astype(jnp.float32)
    runs_ref[...] = tags_f[...].T[KVW - LAT:KVW - LAT + 8, :].astype(jnp.int32)
    for t in twins:
        t.wait_recv()
    for s in sent:
        s.wait_send()


N_GATHER = len(PARTS) * (3 + 12 + 8 + 1 + 8 + 2 + 4)


def gather(positions, latent):
    return pl.pallas_call(
        gather_kernel,
        out_shape=(jax.ShapeDtypeStruct((4, 4, 4, 2, 32, PAD), jnp.bfloat16), jax.ShapeDtypeStruct((8, 128), jnp.int32)),
        in_specs=[pl.BlockSpec(memory_space=pltpu.SMEM), pl.BlockSpec(memory_space=pltpu.VMEM)],
        out_specs=(pl.BlockSpec(memory_space=pltpu.HBM), pl.BlockSpec(memory_space=pltpu.VMEM)),
        scratch_shapes=[
            pltpu.VMEM((32, PAD), jnp.bfloat16),
            pltpu.VMEM((4, 4, 4, 16, 128), jnp.bfloat16),
            pltpu.VMEM((128, 128), jnp.float32),
            pltpu.SemaphoreType.DMA,
            pltpu.SemaphoreType.DMA((N_GATHER,)),
            pltpu.SemaphoreType.DMA((N_GATHER,)),
        ],
        compiler_params=pltpu.CompilerParams(collective_id=0, has_side_effects=True),
        cost_estimate=pl.CostEstimate(flops=0, bytes_accessed=10 * 2**20, transcendentals=0),
        name="gather_latent",
    )(positions, latent)


def dropped(axis, done):
    return axis - sum(1 for a in done if a < axis)


def at(ref, dim, value, rows=None):
    index = [slice(None)] * dim + [value]
    view = ref.at[tuple(index)]
    if rows is not None:
        lead = len(view.shape) - 2
        view = view.at[tuple([slice(None)] * lead + [pl.ds(*rows)])]
    return view


def scatter_kernel(part_ref, ds_ref, keys_ref, out_ref, qg_ref, mine, theirs, keep, wire, relay, landed,
                   keys, keys_t, ds_in, qg_t, qg_out, sem, kt_sem, ds_sem, qg_sem, send, recv):
    place, core = coords()
    load_keys = pltpu.make_async_copy(keys_ref, keys, kt_sem)
    load_keys.start()

    def load_ds(i):
        return pltpu.make_async_copy(ds_ref.at[i // PIECES, pl.ds(lax.rem(i, PIECES) * PIECE, PIECE)], ds_in.at[lax.rem(i, 2)], ds_sem.at[lax.rem(i, 2)])

    load_ds(0).start()

    def slice_of_work(i, _):
        @pl.when(i + 1 < SLICES)
        def _():
            load_ds(i + 1).start()
        load_ds(i).wait()
        c, k = i // PIECES, lax.rem(i, PIECES)

        @pl.when(k == 0)
        def _():
            qg_t[...] = jnp.zeros_like(qg_t)
        qg_t[...] += jnp.dot(keys_t[:, pl.ds(pl.multiple_of(k * PIECE, PIECE), PIECE)], ds_in[lax.rem(i, 2)], preferred_element_type=jnp.float32)

        @pl.when(k == PIECES - 1)
        def _():
            row = pl.multiple_of((c // 2) * RUN, RUN)
            for h in range(0, GROUP, 2):
                a = qg_t[:, h * RUN:h * RUN + 2 * RUN].T.astype(jnp.bfloat16)
                lane = pl.multiple_of(lax.rem(c, 2) * (GROUP * KVW) + h * KVW, 128)
                qg_out[pl.ds(row, RUN), pl.ds(lane, 2 * KVW)] = jnp.concatenate([a[:RUN], a[RUN:]], axis=1)
        return 0

    done_work = [0]

    def work(n):
        first = done_work[0]
        done_work[0] += n
        lax.fori_loop(first, first + n, slice_of_work, 0)

    greet(place, core, True)
    count = [0]
    sent = []

    def copy(src, dst, dev):
        i = count[0]
        count[0] += 1
        c = pltpu.make_async_remote_copy(src, dst, send.at[i], recv.at[i], device_id=dev, device_id_type=MESH)
        c.start()
        sent.append(c)
        return c

    sibling = device(place, 1 - core)
    swaps, loads = [], []
    for n, (order, lane, width) in enumerate(SUM_PARTS):
        other = part_ref.at[:, :, :, pl.ds(32 * (1 - core), 32), pl.ds(lane, width)]
        swaps.append(copy(other, theirs[n], sibling))
        load = pltpu.make_async_copy(part_ref.at[:, :, :, pl.ds(32 * core, 32), pl.ds(lane, width)], mine[n], sem.at[n])
        load.start()
        loads.append(load)

    load_keys.wait()

    def turn(j, _):
        o = pl.multiple_of(j * 256, 256)
        keys_t[:, pl.ds(o, 256)] = keys[pl.ds(o, 256), :KVW].T
        return 0

    lax.fori_loop(0, TOKENS // 256, turn, 0)
    work(PLAN[0])
    halves = ((0, 16), (16, 16))

    def parts(phase):
        for n, (order, lane, width) in enumerate(SUM_PARTS):
            axis = order[phase]
            yield n, axis, dropped(axis, order[:phase]), place[axis], lane, width

    started = []
    for n, axis, dim, me, lane, width in parts(0):
        k, w, rl, ld = keep[n][0], wire[n][0], relay[n], landed[n][0]
        right, left, opp = (lax.rem(me + i, 4) for i in (1, 3, 2))
        rdev, ldev = device(moved(place, axis, 1), core), device(moved(place, axis, 3), core)
        loads[n].wait()
        swaps[n].wait_recv()

        def fill(v):
            at(k, dim, v)[...] = at(mine[n], dim, v)[...].astype(jnp.float32) + at(theirs[n], dim, v)[...].astype(jnp.float32)

        fill(opp)
        at(w, dim, opp)[...] = at(k, dim, opp)[...].astype(w.dtype)
        c0 = copy(at(w, dim, opp, halves[0]), rl.at[0], rdev)
        c1 = copy(at(w, dim, opp, halves[1]), rl.at[1], ldev)
        fill(right)
        at(w, dim, right, halves[1])[...] = at(k, dim, right, halves[1])[...].astype(w.dtype)
        c2 = copy(at(w, dim, right, halves[1]), ld.at[0, 1], rdev)
        fill(left)
        at(w, dim, left, halves[0])[...] = at(k, dim, left, halves[0])[...].astype(w.dtype)
        c3 = copy(at(w, dim, left, halves[0]), ld.at[1, 0], ldev)
        fill(me)
        started.append((c0, c1, c2, c3))
        work(PLAN[1])
    ended = []
    for n, axis, dim, me, lane, width in parts(0):
        k, w, rl, ld = keep[n][0], wire[n][0], relay[n], landed[n][0]
        right, left = lax.rem(me + 1, 4), lax.rem(me + 3, 4)
        rdev, ldev = device(moved(place, axis, 1), core), device(moved(place, axis, 3), core)
        c0, c1, c2, c3 = started[n]
        c0.wait_recv()
        at(w, dim, right, halves[0])[...] = (at(k, dim, right, halves[0])[...] + rl[0].astype(jnp.float32)).astype(w.dtype)
        c4 = copy(at(w, dim, right, halves[0]), ld.at[0, 0], rdev)
        c1.wait_recv()
        at(w, dim, left, halves[1])[...] = (at(k, dim, left, halves[1])[...] + rl[1].astype(jnp.float32)).astype(w.dtype)
        c5 = copy(at(w, dim, left, halves[1]), ld.at[1, 1], ldev)
        ended.append((c2, c3, c4, c5))
    work(PLAN[2])
    going = []
    for phase in (1, 2):
        for n, axis, dim, me, lane, width in parts(phase):
            if phase == 1:
                for c in ended[n]:
                    c.wait_recv()
                ld = landed[n][0]
                was = list(parts(0))[n]
                for h in (0, 1):
                    keep[n][1].at[:, :, pl.ds(*halves[h])][...] = (at(keep[n][0], was[2], was[3], halves[h])[...] + ld[0, h].astype(jnp.float32)) + ld[1, h].astype(jnp.float32)
            else:
                for c in going[n]:
                    c.wait_recv()
                ld = landed[n][1]
                was = list(parts(1))[n]
                keep[n][2][...] = (at(keep[n][1], was[2], was[3])[...] + ld[0].astype(jnp.float32)) + (ld[1].astype(jnp.float32) + ld[2].astype(jnp.float32))
            k, w, ld = keep[n][phase], wire[n][phase], landed[n][phase]
            sends = []
            for slot, by in enumerate((2, 1, 3)):
                v = lax.rem(me + by, 4)
                at(w, dim, v)[...] = at(k, dim, v)[...].astype(w.dtype)
                sends.append(copy(at(w, dim, v), ld.at[slot], device(moved(place, axis, by), core)))
            if phase == 1:
                going.append(sends)
            else:
                going[n] = sends
        work(PLAN[1 + 2 * phase])
        if phase == 2:
            put = pltpu.make_async_copy(qg_out, qg_ref, qg_sem)
            put.start()
    for n, axis, dim, me, lane, width in parts(2):
        for c in going[n]:
            c.wait_recv()
        ld = landed[n][2]
        total = (at(keep[n][2], 0, me)[...] + ld[0]) + (ld[1] + ld[2])
        real = min(width, KVW - lane)
        out_ref[:, pl.ds(lane, real)] = total[:, :real]
    put.wait()
    for s in sent:
        s.wait_send()


N_SCATTER = len(SUM_PARTS) * (1 + 6 + 3 + 3)
WIRES = (jnp.bfloat16, jnp.bfloat16, jnp.float32)


def scatter(part, ds, keys):
    V, f32, bf16 = pltpu.VMEM, jnp.float32, jnp.bfloat16
    mine = [V((4, 4, 4, 32, w), bf16) for _, _, w in SUM_PARTS]
    keep = [[V((4,) * (3 - p) + (32, w), f32) for p in range(3)] for _, _, w in SUM_PARTS]
    wire = [[V((4,) * (3 - p) + (32, w), WIRES[p]) for p in range(3)] for _, _, w in SUM_PARTS]
    relay = [V((2, 4, 4, 16, w), WIRES[0]) for _, _, w in SUM_PARTS]
    landed = [[V((2, 2, 4, 4, 16, w), WIRES[0]), V((3, 4, 32, w), WIRES[1]), V((3, 32, w), WIRES[2])] for _, _, w in SUM_PARTS]
    return pl.pallas_call(
        scatter_kernel,
        out_shape=(jax.ShapeDtypeStruct((32, KVW), f32), jax.ShapeDtypeStruct((2 * RUN, HEADS * KVW), bf16)),
        in_specs=[pl.BlockSpec(memory_space=pltpu.HBM)] * 3,
        out_specs=(pl.BlockSpec(memory_space=pltpu.VMEM), pl.BlockSpec(memory_space=pltpu.HBM)),
        scratch_shapes=[
            mine, list(mine), keep, wire, relay, landed,
            V((TOKENS, PAD), bf16), V((KVW, TOKENS), bf16), V((2, PIECE, ROWS), bf16), V((KVW, ROWS), f32), V((2 * RUN, HEADS * KVW), bf16),
            pltpu.SemaphoreType.DMA((len(SUM_PARTS),)), pltpu.SemaphoreType.DMA, pltpu.SemaphoreType.DMA((2,)), pltpu.SemaphoreType.DMA,
            pltpu.SemaphoreType.DMA((N_SCATTER,)),
            pltpu.SemaphoreType.DMA((N_SCATTER,)),
        ],
        compiler_params=pltpu.CompilerParams(collective_id=1, has_side_effects=True, vmem_limit_bytes=56 * 2**20),
        cost_estimate=pl.CostEstimate(flops=10**10, bytes_accessed=3 * 10**7, transcendentals=0),
        name="scatter_latent_grad",
    )(part, ds, keys)


def attend_kernel(pos_ref, runs_ref, q_ref, do_ref, kg_ref, ds_ref, keys_ref, part_ref,
                  chip_of, keys, acc, exps, gws, tops, qs, qs_t, dos, dos_t, q_in, do_in, ds_out,
                  key_sem, in_sem, out_sem, ds_sem):
    f32, bf16 = jnp.float32, jnp.bfloat16
    copy_keys = pltpu.make_async_copy(keys, keys_ref, out_sem.at[1])

    def inputs(c):
        row = pl.ds(pl.multiple_of((c // 2) * RUN, RUN), RUN)
        out = []
        for i, (ref, to, width) in enumerate(((q_ref, q_in, GROUP * KVW), (do_ref, do_in, GROUP * LAT))):
            lane = pl.ds(pl.multiple_of(lax.rem(c, 2) * width, 128), width)
            out.append(pltpu.make_async_copy(ref.at[row, lane], to.at[row, lane], in_sem.at[i, c]))
        return out

    def take(c, _):
        for copy in inputs(c):
            copy.start()
        return 0

    take(0, 0)

    def place(chip, _):
        chip_of[runs_ref[0, chip]] = chip
        return 0

    lax.fori_loop(0, RUNS, place, 0)

    def fetch(j, _):
        pltpu.make_async_copy(kg_ref.at[chip_of[j]], keys.at[pl.ds(j * RUN, RUN)], key_sem.at[j // (BIG // RUN)]).start()
        return 0

    lax.fori_loop(0, BIG // RUN, fetch, 0)
    lax.fori_loop(BIG // RUN, RUNS, fetch, 0)
    lax.fori_loop(1, CHUNKS, take, 0)

    def await_keys(t, _):
        tile = keys.at[pl.ds(pl.multiple_of(t * BIG, BIG), BIG)]
        pltpu.make_async_copy(tile, tile, key_sem.at[t]).wait()
        return 0

    acc[...] = jnp.zeros_like(acc)
    qs[:, LAT:] = jnp.zeros((ROWS, PAD - LAT), bf16)

    def chunk(c, _):
        for copy in inputs(c):
            copy.wait()
        half, block, slot = lax.rem(c, 2), c // 2, lax.rem(c, 2)
        run = pos_ref[block * RUN] // RUN
        row = pl.multiple_of(block * RUN, RUN)
        for h in range(0, GROUP, 2):
            v = q_in[pl.ds(row, RUN), pl.ds(pl.multiple_of(half * (GROUP * KVW) + h * KVW, 128), 2 * KVW)]
            qs[h * RUN:h * RUN + RUN, :KVW] = v[:, :KVW]
            qs[h * RUN + RUN:h * RUN + 2 * RUN, :KVW] = v[:, KVW:]
            d = do_in[pl.ds(row, RUN), pl.ds(pl.multiple_of(half * (GROUP * LAT) + h * LAT, 128), 2 * LAT)]
            dos[h * RUN:h * RUN + RUN, :] = d[:, :LAT]
            dos[h * RUN + RUN:h * RUN + 2 * RUN, :] = d[:, LAT:]
        qs_t[...] = qs[...].T
        dos_t[...] = dos[...].T
        full = run // (SMALL // RUN)
        huge = full // (HUGE // SMALL)
        rest = lax.rem(full, HUGE // SMALL)
        big = rest // (BIG // SMALL)
        over = lax.rem(rest, BIG // SMALL)
        last = full - over

        def scan(u, size, masked, carry):
            m, l, d = carry

            @pl.when(c == 0)
            def _():
                for i in range(max(size // BIG, 1)):
                    await_keys(u // (BIG // SMALL) + i, 0)
            o = pl.multiple_of(u * SMALL, SMALL)
            tile = keys[pl.ds(o, size), :]
            s = jnp.dot(tile, qs_t[...], preferred_element_type=f32)
            g = jnp.dot(tile[:, :LAT], dos_t[...], preferred_element_type=f32)
            if masked:
                key = lax.broadcasted_iota(jnp.int32, (size, ROWS), 0)
                tok = lax.broadcasted_iota(jnp.int32, (size, ROWS), 1) % RUN
                s = jnp.where(key - tok <= run * RUN - o, s, MASKED)
            s = s * TO_BASE_2
            top = jnp.maximum(m, jnp.max(s, axis=0, keepdims=True))
            e = jnp.exp2(s - top)
            exps[pl.ds(o, size), :] = e
            gws[pl.ds(o, size), :] = g
            tops[pl.ds(pl.multiple_of(u * 8, 8), 8), :] = jnp.broadcast_to(top, (8, ROWS))
            a = jnp.exp2(m - top)
            return top, l * a + jnp.sum(e, axis=0, keepdims=True), d * a + jnp.sum(e * g, axis=0, keepdims=True)

        start = (jnp.full((1, ROWS), MASKED, f32), jnp.zeros((1, ROWS), f32), jnp.zeros((1, ROWS), f32))
        carry = lax.fori_loop(0, huge, lambda t, s: scan(t * (HUGE // SMALL), HUGE, False, s), start)
        carry = lax.fori_loop(0, big, lambda t, s: scan(huge * (HUGE // SMALL), BIG, False, s), carry)
        m, l, d = lax.switch(over, [lambda n=n: scan(last, n * SMALL, True, carry) for n in range(1, BIG // SMALL + 1)])

        @pl.when(c == 0)
        def _():
            lax.fori_loop(last // (BIG // SMALL) + 1, TOKENS // BIG, await_keys, 0)
            copy_keys.start()
        share = 1.0 / l
        delta = d * share

        @pl.when(c >= 2)
        def _():
            pltpu.make_async_copy(ds_out.at[slot], ds_ref.at[c], ds_sem.at[slot]).wait()

        def leave_ds(k, _):
            span = pl.ds(pl.multiple_of(k * BIG, BIG), BIG)
            pltpu.make_async_copy(ds_out.at[slot, span], ds_ref.at[c, span], ds_sem.at[slot]).start()
            return 0

        def back(u, size):
            o = pl.multiple_of(u * SMALL, SMALL)
            span = pl.ds(o, size)
            w = exps[span, :] * (jnp.exp2(tops[pl.ds(pl.multiple_of(u * 8, 8), 8), :][:1] - m) * share)
            ds = (w * ((gws[span, :] - delta) * SCALE)).astype(bf16)
            ds_out[slot, span, :] = ds
            nt = (((1,), (1,)), ((), ()))
            acc[:, span] += lax.dot_general(qs_t[:KVW], ds, nt, preferred_element_type=f32)
            acc[:LAT, span] += lax.dot_general(dos_t[...], w.astype(bf16), nt, preferred_element_type=f32)
            for k in range(max(size // BIG, 1)):
                leave_ds(u // (BIG // SMALL) + k, 0)
            return 0

        def blank(u, _):
            ds_out[slot, pl.ds(pl.multiple_of(u * SMALL, SMALL), SMALL), :] = jnp.zeros((SMALL, ROWS), bf16)
            return 0

        lax.fori_loop(full + 1, TOKENS // SMALL, blank, 0)
        lax.fori_loop(last // (BIG // SMALL) + 1, QUARTERS, leave_ds, 0)
        lax.fori_loop(0, huge, lambda t, _: back(t * (HUGE // SMALL), HUGE), 0)
        lax.fori_loop(0, big, lambda t, _: back(huge * (HUGE // SMALL), BIG), 0)
        lax.switch(over, [lambda n=n: back(last, n * SMALL) for n in range(1, BIG // SMALL + 1)])

        return 0

    lax.fori_loop(0, CHUNKS, chunk, 0)
    copy_keys.wait()

    def leave(j, _):
        o = pl.multiple_of(j * 256, 256)
        keys[pl.ds(o, 256), :KVW] = acc[:, pl.ds(o, 256)].astype(bf16).T
        for i in range(4):
            pltpu.make_async_copy(keys.at[pl.ds(o + i * RUN, RUN)], part_ref.at[chip_of[j * 4 + i]], out_sem.at[0]).start()
        return 0

    lax.fori_loop(0, TOKENS // 256, leave, 0)
    for slot in range(2):
        pltpu.make_async_copy(ds_out.at[slot], ds_ref.at[0], ds_sem.at[slot]).wait()
    pltpu.make_async_copy(keys, keys, out_sem.at[0]).wait()


def attend(positions, runs, query, out_grad, gathered):
    V, f32, bf16 = pltpu.VMEM, jnp.float32, jnp.bfloat16
    return pl.pallas_call(
        attend_kernel,
        out_shape=(jax.ShapeDtypeStruct((CHUNKS, TOKENS, ROWS), bf16), jax.ShapeDtypeStruct((TOKENS, PAD), bf16),
                   jax.ShapeDtypeStruct((RUNS, RUN, PAD), bf16)),
        in_specs=[pl.BlockSpec(memory_space=pltpu.SMEM)] * 2 + [pl.BlockSpec(memory_space=pltpu.HBM)] * 3,
        out_specs=(pl.BlockSpec(memory_space=pltpu.HBM),) * 3,
        scratch_shapes=[
            pltpu.SMEM((RUNS,), jnp.int32),
            V((TOKENS, PAD), bf16), V((KVW, TOKENS), f32),
            V((TOKENS, ROWS), f32), V((TOKENS, ROWS), f32), V((TOKENS // SMALL * 8, ROWS), f32),
            V((ROWS, PAD), bf16), V((PAD, ROWS), bf16), V((ROWS, LAT), bf16), V((LAT, ROWS), bf16),
            V((2 * RUN, HEADS * KVW), bf16), V((2 * RUN, HEADS * LAT), bf16), V((2, TOKENS, ROWS), bf16),
            pltpu.SemaphoreType.DMA((TOKENS // BIG,)), pltpu.SemaphoreType.DMA((2, CHUNKS)), pltpu.SemaphoreType.DMA((2,)), pltpu.SemaphoreType.DMA((2,)),
        ],
        compiler_params=pltpu.CompilerParams(vmem_limit_bytes=62 * 2**20),
        cost_estimate=pl.CostEstimate(flops=46 * 10**9, bytes_accessed=2 * 10**7, transcendentals=10**7),
        name="attend",
    )(positions, runs, query, out_grad, gathered)


def settle_kernel(qg_in, lg_in, qg_ref, lg_ref, qg_buf, lg_buf, sem):
    pieces = [(qg_in.at[pl.ds(i * 16, 16)], qg_buf.at[pl.ds(i * 16, 16)], qg_ref.at[pl.ds(i * 16, 16)]) for i in range(8)]
    pieces.append((lg_in, lg_buf, lg_ref))
    loads = [pltpu.make_async_copy(a, b, sem.at[0, i]) for i, (a, b, _) in enumerate(pieces)]
    stores = [pltpu.make_async_copy(b, c, sem.at[1, i]) for i, (_, b, c) in enumerate(pieces)]
    for load in loads:
        load.start()
    for load, store in zip(loads, stores):
        load.wait()
        store.start()
    for store in stores:
        store.wait()


def settle(query_grad, latent_grad):
    return pl.pallas_call(
        settle_kernel,
        out_shape=(jax.ShapeDtypeStruct(query_grad.shape, query_grad.dtype), jax.ShapeDtypeStruct(latent_grad.shape, latent_grad.dtype)),
        in_specs=[pl.BlockSpec(memory_space=pltpu.HBM), pl.BlockSpec(memory_space=pl.ANY)],
        out_specs=(pl.BlockSpec(memory_space=pltpu.HBM),) * 2,
        scratch_shapes=[pltpu.VMEM(query_grad.shape, query_grad.dtype), pltpu.VMEM(latent_grad.shape, latent_grad.dtype), pltpu.SemaphoreType.DMA((2, 9))],
        cost_estimate=pl.CostEstimate(flops=0, bytes_accessed=5 * 10**6, transcendentals=0),
        name="settle",
    )(query_grad, latent_grad)


def per_device(query, latent, out_grad, positions):
    gathered, runs = gather(positions, latent)
    ds, keys, part = attend(positions, runs, query, out_grad, gathered.reshape(RUNS, RUN, PAD))
    latent_grad, query_grad = scatter(part.reshape(4, 4, 4, RUN, PAD), ds, keys)
    return settle(query_grad, latent_grad)


def solution(mesh):
    return jax.shard_map(
        per_device,
        mesh=mesh,
        in_specs=(P("seq", "tp"), P(("seq", "tp"), None), P("seq", "tp"), P("seq")),
        out_specs=(P("seq", "tp"), P(("seq", "tp"), None)),
        check_vma=False,
    )
```

```python
import math

import jax, jax.numpy as jnp
from jax import lax
from jax.experimental import pallas as pl
from jax.experimental.pallas import tpu as pltpu
from jax.sharding import PartitionSpec as P

LAT=512; KVW=576; PAD=640
SCALE = 192.0 ** -0.5
TO_BASE_2 = SCALE * math.log2(math.e)
MASKED = -1e30
TOKENS = 4096
RUN = 64
RUNS = TOKENS // RUN
HEADS = 16
GROUP = 8
ROWS = GROUP * RUN
HUGE, BIG, PART, SMALL = 2048, 1024, 512, 256
CHUNKS = 2 * HEADS // GROUP
QUARTERS = TOKENS // BIG
PIECE = 2048
PIECES = TOKENS // PIECE
SLICES = CHUNKS * PIECES
PLAN = (0, 1, 3, 3, 0, 1)
MESH = pl.DeviceIdType.MESH
PARTS = (((0, 1, 2), 0, 256), ((1, 2, 0), 256, 256), ((2, 0, 1), 512, 128))
SUM_PARTS = (((0, 2, 1), 0, 256), ((1, 2, 0), 256, 256), ((2, 1, 0), 512, 128))


def coords():
    seq, tp = lax.axis_index("seq"), lax.axis_index("tp")
    x = lax.rem(seq, 4)
    z = lax.rem(seq // 4, 2) * 2 + tp // 2
    y = seq // 8
    return [x, y, z], lax.rem(tp, 2)


def device(place, core):
    x, y, z = place
    return ((y * 2 + z // 2) * 4 + x, lax.rem(z, 2) * 2 + core)


def moved(place, axis, by):
    out = list(place)
    out[axis] = lax.rem(place[axis] + by, 4)
    return out


def greet(place, core, opposite=False):
    barrier = pltpu.get_barrier_semaphore()
    steps = (1, 2, 3) if opposite else (1, 3)
    for axis in range(3):
        for by in steps:
            pl.semaphore_signal(barrier, inc=1, device_id=device(moved(place, axis, by), core), device_id_type=MESH)
    pl.semaphore_signal(barrier, inc=1, device_id=device(place, 1 - core), device_id_type=MESH)
    pl.semaphore_wait(barrier, 3 * len(steps) + 1)


def gather_kernel(pos_ref, lat_ref, out_ref, runs_ref, own, tags, tags_f, sem, send, recv):
    place, core = coords()
    run = pos_ref[lax.rem(place[2], 2) * 64] // 64
    own[:, :KVW] = lat_ref[...]
    own[:, KVW:] = jnp.full((32, PAD - KVW), run.astype(jnp.float32)).astype(jnp.bfloat16)
    put = pltpu.make_async_copy(own, out_ref.at[place[0], place[1], place[2], core], sem)
    put.start()
    greet(place, core, True)
    sent = []

    def copy(ref, dev, source=None):
        i = len(sent)
        c = pltpu.make_async_remote_copy(ref if source is None else source, ref, send.at[i], recv.at[i], device_id=dev, device_id_type=MESH)
        c.start()
        sent.append(c)
        return c

    def shards(order, lane, width, at1, at2, at3, rows=(0, 32)):
        at = [None] * 3
        for axis, v in zip(order, (at1, at2, at3)):
            at[axis] = pl.ds(0, 4) if v is None else lax.rem(place[axis] + v, 4)
        return out_ref.at[at[0], at[1], at[2], core, pl.ds(*rows), pl.ds(lane, width)]

    sibling = device(place, 1 - core)
    twins = []
    one, two, three = {}, {}, {}
    steps = (1, 3, 2)

    def spread(p, d1):
        order, lane, width = PARTS[p]
        for by in steps:
            two[p, d1, by] = copy(shards(order, lane, width, d1, 0, 0), device(moved(place, order[1], by), core), None if d1 else own.at[:, pl.ds(lane, width)])

    def shift(p, d2):
        order, lane, width = PARTS[p]
        for by in (1, 3):
            three[p, d2, by] = copy(shards(order, lane, width, None, d2, 0), device(moved(place, order[2], by), core))

    def forward(p, d2):
        order, lane, width = PARTS[p]
        three[p, d2, 1].wait_recv()
        three[p, d2, 4] = copy(shards(order, lane, width, None, d2, 3, (0, 16)), device(moved(place, order[2], 1), core))
        three[p, d2, 3].wait_recv()
        three[p, d2, 5] = copy(shards(order, lane, width, None, d2, 1, (16, 16)), device(moved(place, order[2], 3), core))

    def arrive(p, d2):
        for d1 in (0, 1, 3, 2):
            two[p, d1, {3: 1, 1: 3, 2: 2}[d2]].wait_recv()

    n = range(len(PARTS))
    for p in n:
        order, lane, width = PARTS[p]
        for by in steps:
            one[p, by] = copy(shards(order, lane, width, 0, 0, 0), device(moved(place, order[0], by), core), own.at[:, pl.ds(lane, width)])
    for p in n:
        spread(p, 0)
    for by in steps:
        for p in n:
            one[p, by].wait_recv()
            spread(p, {1: 3, 3: 1, 2: 2}[by])
    put.wait()
    for p in n:
        shift(p, 0)
    for d2 in (3, 1, 2):
        for p in n:
            arrive(p, d2)
            shift(p, d2)
    for p in n:
        order, lane, width = PARTS[p]
        twins.append(copy(shards(order, lane, width, None, None, 0), sibling))
    for d2 in (0, 3, 1, 2):
        for p in n:
            forward(p, d2)
    for p in n:
        order, lane, width = PARTS[p]
        twins.append(copy(shards(order, lane, width, None, None, 3), sibling))
        twins.append(copy(shards(order, lane, width, None, None, 1), sibling))
    tagged = [p for p in n if PARTS[p][1] == LAT][0]
    for p in (tagged, *[p for p in n if p != tagged]):
        order, lane, width = PARTS[p]
        for d2 in (0, 3, 1, 2):
            three[p, d2, 4].wait_recv()
            three[p, d2, 5].wait_recv()
            twins.append(copy(shards(order, lane, width, None, d2, 2), sibling))
        if p == tagged:
            load_tags = pltpu.make_async_copy(out_ref.at[:, :, :, core, pl.ds(0, 16), pl.ds(LAT, 128)], tags, sem)
            load_tags.start()
    load_tags.wait()
    tags_f[...] = jnp.zeros_like(tags_f)
    tags_f[:RUNS, :] = tags[:, :, :, 0, :].reshape(RUNS, 128).astype(jnp.float32)
    runs_ref[...] = tags_f[...].T[KVW - LAT:KVW - LAT + 8, :].astype(jnp.int32)
    for t in twins:
        t.wait_recv()
    for s in sent:
        s.wait_send()


N_GATHER = len(PARTS) * (3 + 12 + 8 + 1 + 8 + 2 + 4)


def gather(positions, latent):
    return pl.pallas_call(
        gather_kernel,
        out_shape=(jax.ShapeDtypeStruct((4, 4, 4, 2, 32, PAD), jnp.bfloat16), jax.ShapeDtypeStruct((8, 128), jnp.int32)),
        in_specs=[pl.BlockSpec(memory_space=pltpu.SMEM), pl.BlockSpec(memory_space=pltpu.VMEM)],
        out_specs=(pl.BlockSpec(memory_space=pltpu.HBM), pl.BlockSpec(memory_space=pltpu.VMEM)),
        scratch_shapes=[
            pltpu.VMEM((32, PAD), jnp.bfloat16),
            pltpu.VMEM((4, 4, 4, 16, 128), jnp.bfloat16),
            pltpu.VMEM((128, 128), jnp.float32),
            pltpu.SemaphoreType.DMA,
            pltpu.SemaphoreType.DMA((N_GATHER,)),
            pltpu.SemaphoreType.DMA((N_GATHER,)),
        ],
        compiler_params=pltpu.CompilerParams(collective_id=0, has_side_effects=True),
        cost_estimate=pl.CostEstimate(flops=0, bytes_accessed=10 * 2**20, transcendentals=0),
        name="gather_latent",
    )(positions, latent)


def dropped(axis, done):
    return axis - sum(1 for a in done if a < axis)


def at(ref, dim, value, rows=None):
    index = [slice(None)] * dim + [value]
    view = ref.at[tuple(index)]
    if rows is not None:
        lead = len(view.shape) - 2
        view = view.at[tuple([slice(None)] * lead + [pl.ds(*rows)])]
    return view


def scatter_kernel(part_ref, ds_ref, keys_ref, out_ref, qg_ref, mine, theirs, keep, wire, relay, landed,
                   keys, keys_t, ds_in, qg_t, qg_out, sem, kt_sem, ds_sem, qg_sem, send, recv):
    place, core = coords()
    load_keys = pltpu.make_async_copy(keys_ref, keys, kt_sem)

    def load_ds(i):
        return pltpu.make_async_copy(ds_ref.at[i // PIECES, pl.ds(lax.rem(i, PIECES) * PIECE, PIECE)], ds_in.at[lax.rem(i, 2)], ds_sem.at[lax.rem(i, 2)])

    def slice_of_work(i, _):
        @pl.when(i + 1 < SLICES)
        def _():
            load_ds(i + 1).start()
        load_ds(i).wait()
        c, k = i // PIECES, lax.rem(i, PIECES)

        @pl.when(k == 0)
        def _():
            qg_t[...] = jnp.zeros_like(qg_t)
        qg_t[...] += jnp.dot(keys_t[:, pl.ds(pl.multiple_of(k * PIECE, PIECE), PIECE)], ds_in[lax.rem(i, 2)], preferred_element_type=jnp.float32)

        @pl.when(k == PIECES - 1)
        def _():
            row = pl.multiple_of((c // 2) * RUN, RUN)
            for h in range(0, GROUP, 2):
                a = qg_t[:, h * RUN:h * RUN + 2 * RUN].T.astype(jnp.bfloat16)
                lane = pl.multiple_of(lax.rem(c, 2) * (GROUP * KVW) + h * KVW, 128)
                qg_out[pl.ds(row, RUN), pl.ds(lane, 2 * KVW)] = jnp.concatenate([a[:RUN], a[RUN:]], axis=1)
        return 0

    done_work = [0]

    def work(n):
        first = done_work[0]
        done_work[0] += n
        lax.fori_loop(first, first + n, slice_of_work, 0)

    greet(place, core, True)
    count = [0]
    sent = []

    def copy(src, dst, dev):
        i = count[0]
        count[0] += 1
        c = pltpu.make_async_remote_copy(src, dst, send.at[i], recv.at[i], device_id=dev, device_id_type=MESH)
        c.start()
        sent.append(c)
        return c

    sibling = device(place, 1 - core)
    swaps, loads = [], []
    for n, (order, lane, width) in enumerate(SUM_PARTS):
        other = part_ref.at[:, :, :, pl.ds(32 * (1 - core), 32), pl.ds(lane, width)]
        swaps.append(copy(other, theirs[n], sibling))
        load = pltpu.make_async_copy(part_ref.at[:, :, :, pl.ds(32 * core, 32), pl.ds(lane, width)], mine[n], sem.at[n])
        load.start()
        loads.append(load)

    load_keys.start()
    load_ds(0).start()

    def turn(j, _):
        o = pl.multiple_of(j * 256, 256)
        keys_t[:, pl.ds(o, 256)] = keys[pl.ds(o, 256), :KVW].T
        return 0

    halves = ((0, 16), (16, 16))

    def parts(phase):
        for n, (order, lane, width) in enumerate(SUM_PARTS):
            axis = order[phase]
            yield n, axis, dropped(axis, order[:phase]), place[axis], lane, width

    started = []
    for n, axis, dim, me, lane, width in parts(0):
        k, w, rl, ld = keep[n][0], wire[n][0], relay[n], landed[n][0]
        right, left, opp = (lax.rem(me + i, 4) for i in (1, 3, 2))
        rdev, ldev = device(moved(place, axis, 1), core), device(moved(place, axis, 3), core)
        loads[n].wait()
        swaps[n].wait_recv()

        def fill(v):
            at(k, dim, v)[...] = at(mine[n], dim, v)[...].astype(jnp.float32) + at(theirs[n], dim, v)[...].astype(jnp.float32)

        fill(opp)
        at(w, dim, opp)[...] = at(k, dim, opp)[...].astype(w.dtype)
        c0 = copy(at(w, dim, opp, halves[0]), rl.at[0], rdev)
        c1 = copy(at(w, dim, opp, halves[1]), rl.at[1], ldev)
        fill(right)
        at(w, dim, right, halves[1])[...] = at(k, dim, right, halves[1])[...].astype(w.dtype)
        c2 = copy(at(w, dim, right, halves[1]), ld.at[0, 1], rdev)
        fill(left)
        at(w, dim, left, halves[0])[...] = at(k, dim, left, halves[0])[...].astype(w.dtype)
        c3 = copy(at(w, dim, left, halves[0]), ld.at[1, 0], ldev)
        fill(me)
        started.append((c0, c1, c2, c3))
        if n == 2:
            load_keys.wait()
            lax.fori_loop(0, TOKENS // 256, turn, 0)
        work(PLAN[1 if n == 2 else 0])
    ended = []
    for n, axis, dim, me, lane, width in parts(0):
        k, w, rl, ld = keep[n][0], wire[n][0], relay[n], landed[n][0]
        right, left = lax.rem(me + 1, 4), lax.rem(me + 3, 4)
        rdev, ldev = device(moved(place, axis, 1), core), device(moved(place, axis, 3), core)
        c0, c1, c2, c3 = started[n]
        c0.wait_recv()
        at(w, dim, right, halves[0])[...] = (at(k, dim, right, halves[0])[...] + rl[0].astype(jnp.float32)).astype(w.dtype)
        c4 = copy(at(w, dim, right, halves[0]), ld.at[0, 0], rdev)
        c1.wait_recv()
        at(w, dim, left, halves[1])[...] = (at(k, dim, left, halves[1])[...] + rl[1].astype(jnp.float32)).astype(w.dtype)
        c5 = copy(at(w, dim, left, halves[1]), ld.at[1, 1], ldev)
        ended.append((c2, c3, c4, c5))
    work(PLAN[2])
    going = []
    for phase in (1, 2):
        for n, axis, dim, me, lane, width in parts(phase):
            if phase == 1:
                for c in ended[n]:
                    c.wait_recv()
                ld = landed[n][0]
                was = list(parts(0))[n]
                for h in (0, 1):
                    keep[n][1].at[:, :, pl.ds(*halves[h])][...] = (at(keep[n][0], was[2], was[3], halves[h])[...] + ld[0, h].astype(jnp.float32)) + ld[1, h].astype(jnp.float32)
            else:
                for c in going[n]:
                    c.wait_recv()
                ld = landed[n][1]
                was = list(parts(1))[n]
                keep[n][2][...] = (at(keep[n][1], was[2], was[3])[...] + ld[0].astype(jnp.float32)) + (ld[1].astype(jnp.float32) + ld[2].astype(jnp.float32))
            k, w, ld = keep[n][phase], wire[n][phase], landed[n][phase]
            sends = []
            for slot, by in enumerate((2, 1, 3)):
                v = lax.rem(me + by, 4)
                at(w, dim, v)[...] = at(k, dim, v)[...].astype(w.dtype)
                sends.append(copy(at(w, dim, v), ld.at[slot], device(moved(place, axis, by), core)))
            if phase == 1:
                going.append(sends)
            else:
                going[n] = sends
        work(PLAN[1 + 2 * phase])
        if phase == 2:
            put = pltpu.make_async_copy(qg_out, qg_ref, qg_sem)
            put.start()
    for n, axis, dim, me, lane, width in parts(2):
        for c in going[n]:
            c.wait_recv()
        ld = landed[n][2]
        total = (at(keep[n][2], 0, me)[...] + ld[0]) + (ld[1] + ld[2])
        real = min(width, KVW - lane)
        out_ref[:, pl.ds(lane, real)] = total[:, :real]
    put.wait()
    for s in sent:
        s.wait_send()


N_SCATTER = len(SUM_PARTS) * (1 + 6 + 3 + 3)
WIRES = (jnp.bfloat16, jnp.bfloat16, jnp.float32)


def scatter(part, ds, keys):
    V, f32, bf16 = pltpu.VMEM, jnp.float32, jnp.bfloat16
    mine = [V((4, 4, 4, 32, w), bf16) for _, _, w in SUM_PARTS]
    keep = [[V((4,) * (3 - p) + (32, w), f32) for p in range(3)] for _, _, w in SUM_PARTS]
    wire = [[V((4,) * (3 - p) + (32, w), WIRES[p]) for p in range(3)] for _, _, w in SUM_PARTS]
    relay = [V((2, 4, 4, 16, w), WIRES[0]) for _, _, w in SUM_PARTS]
    landed = [[V((2, 2, 4, 4, 16, w), WIRES[0]), V((3, 4, 32, w), WIRES[1]), V((3, 32, w), WIRES[2])] for _, _, w in SUM_PARTS]
    return pl.pallas_call(
        scatter_kernel,
        out_shape=(jax.ShapeDtypeStruct((32, KVW), f32), jax.ShapeDtypeStruct((2 * RUN, HEADS * KVW), bf16)),
        in_specs=[pl.BlockSpec(memory_space=pltpu.HBM)] * 3,
        out_specs=(pl.BlockSpec(memory_space=pltpu.VMEM), pl.BlockSpec(memory_space=pltpu.HBM)),
        scratch_shapes=[
            mine, list(mine), keep, wire, relay, landed,
            V((TOKENS, PAD), bf16), V((KVW, TOKENS), bf16), V((2, PIECE, ROWS), bf16), V((KVW, ROWS), f32), V((2 * RUN, HEADS * KVW), bf16),
            pltpu.SemaphoreType.DMA((len(SUM_PARTS),)), pltpu.SemaphoreType.DMA, pltpu.SemaphoreType.DMA((2,)), pltpu.SemaphoreType.DMA,
            pltpu.SemaphoreType.DMA((N_SCATTER,)),
            pltpu.SemaphoreType.DMA((N_SCATTER,)),
        ],
        compiler_params=pltpu.CompilerParams(collective_id=1, has_side_effects=True, vmem_limit_bytes=56 * 2**20),
        cost_estimate=pl.CostEstimate(flops=10**10, bytes_accessed=3 * 10**7, transcendentals=0),
        name="scatter_latent_grad",
    )(part, ds, keys)


def attend_kernel(pos_ref, runs_ref, q_ref, do_ref, kg_ref, ds_ref, keys_ref, part_ref,
                  chip_of, keys, acc, exps, gws, tops, qs, qs_t, dos, dos_t, q_in, do_in, ds_out,
                  key_sem, in_sem, out_sem, ds_sem):
    f32, bf16 = jnp.float32, jnp.bfloat16
    copy_keys = pltpu.make_async_copy(keys, keys_ref, out_sem.at[1])

    def inputs(c):
        row = pl.ds(pl.multiple_of((c // 2) * RUN, RUN), RUN)
        out = []
        for i, (ref, to, width) in enumerate(((q_ref, q_in, GROUP * KVW), (do_ref, do_in, GROUP * LAT))):
            lane = pl.ds(pl.multiple_of(lax.rem(c, 2) * width, 128), width)
            out.append(pltpu.make_async_copy(ref.at[row, lane], to.at[row, lane], in_sem.at[i, c]))
        return out

    def take(c, _):
        for copy in inputs(c):
            copy.start()
        return 0

    take(0, 0)

    def place(chip, _):
        chip_of[runs_ref[0, chip]] = chip
        return 0

    lax.fori_loop(0, RUNS, place, 0)

    def fetch(j, _):
        pltpu.make_async_copy(kg_ref.at[chip_of[j]], keys.at[pl.ds(j * RUN, RUN)], key_sem.at[j // (BIG // RUN)]).start()
        return 0

    lax.fori_loop(0, BIG // RUN, fetch, 0)
    lax.fori_loop(BIG // RUN, RUNS, fetch, 0)
    lax.fori_loop(1, CHUNKS, take, 0)

    def await_keys(t, _):
        tile = keys.at[pl.ds(pl.multiple_of(t * BIG, BIG), BIG)]
        pltpu.make_async_copy(tile, tile, key_sem.at[t]).wait()
        return 0

    acc[...] = jnp.zeros_like(acc)
    qs[:, LAT:] = jnp.zeros((ROWS, PAD - LAT), bf16)

    def chunk(c, _):
        for copy in inputs(c):
            copy.wait()
        half, block, slot = lax.rem(c, 2), c // 2, lax.rem(c, 2)
        run = pos_ref[block * RUN] // RUN
        row = pl.multiple_of(block * RUN, RUN)
        for h in range(0, GROUP, 2):
            v = q_in[pl.ds(row, RUN), pl.ds(pl.multiple_of(half * (GROUP * KVW) + h * KVW, 128), 2 * KVW)]
            qs[h * RUN:h * RUN + RUN, :KVW] = v[:, :KVW]
            qs[h * RUN + RUN:h * RUN + 2 * RUN, :KVW] = v[:, KVW:]
            d = do_in[pl.ds(row, RUN), pl.ds(pl.multiple_of(half * (GROUP * LAT) + h * LAT, 128), 2 * LAT)]
            dos[h * RUN:h * RUN + RUN, :] = d[:, :LAT]
            dos[h * RUN + RUN:h * RUN + 2 * RUN, :] = d[:, LAT:]
        qs_t[...] = qs[...].T
        dos_t[...] = dos[...].T
        full = run // (SMALL // RUN)
        huge = full // (HUGE // SMALL)
        rest = lax.rem(full, HUGE // SMALL)
        big = rest // (BIG // SMALL)
        over = lax.rem(rest, BIG // SMALL)
        last = full - over

        def huge_scan(u, carry):
            @pl.when(c == 0)
            def _():
                for i in range(HUGE // BIG):
                    await_keys(u // (BIG // SMALL) + i, 0)
            for i in range(HUGE // PART):
                carry = scan(u + i * (PART // SMALL), PART, False, carry, False)
            return carry

        def scan(u, size, masked, carry, wait=True):
            m, l, d = carry
            if wait:
                @pl.when(c == 0)
                def _():
                    for i in range(max(size // BIG, 1)):
                        await_keys(u // (BIG // SMALL) + i, 0)
            o = pl.multiple_of(u * SMALL, SMALL)
            tile = keys[pl.ds(o, size), :]
            s = jnp.dot(tile, qs_t[...], preferred_element_type=f32)
            g = jnp.dot(tile[:, :LAT], dos_t[...], preferred_element_type=f32)
            if masked:
                key = lax.broadcasted_iota(jnp.int32, (size, ROWS), 0)
                tok = lax.broadcasted_iota(jnp.int32, (size, ROWS), 1) % RUN
                s = jnp.where(key - tok <= run * RUN - o, s, MASKED)
            s = s * TO_BASE_2
            top = jnp.maximum(m, jnp.max(s, axis=0, keepdims=True))
            e = jnp.exp2(s - top)
            exps[pl.ds(o, size), :] = e
            gws[pl.ds(o, size), :] = g
            tops[pl.ds(pl.multiple_of(u * 8, 8), 8), :] = jnp.broadcast_to(top, (8, ROWS))
            a = jnp.exp2(m - top)
            return top, l * a + jnp.sum(e, axis=0, keepdims=True), d * a + jnp.sum(e * g, axis=0, keepdims=True)

        start = (jnp.full((1, ROWS), MASKED, f32), jnp.zeros((1, ROWS), f32), jnp.zeros((1, ROWS), f32))
        carry = lax.fori_loop(0, huge, lambda t, s: huge_scan(t * (HUGE // SMALL), s), start)
        carry = lax.fori_loop(0, big, lambda t, s: scan(huge * (HUGE // SMALL), BIG, False, s), carry)
        m, l, d = lax.switch(over, [lambda n=n: scan(last, n * SMALL, True, carry) for n in range(1, BIG // SMALL + 1)])

        @pl.when(c == 0)
        def _():
            lax.fori_loop(last // (BIG // SMALL) + 1, TOKENS // BIG, await_keys, 0)
            copy_keys.start()
        share = 1.0 / l
        delta = d * share

        @pl.when(c >= 2)
        def _():
            pltpu.make_async_copy(ds_out.at[slot], ds_ref.at[c], ds_sem.at[slot]).wait()

        def leave_ds(k, _):
            span = pl.ds(pl.multiple_of(k * BIG, BIG), BIG)
            pltpu.make_async_copy(ds_out.at[slot, span], ds_ref.at[c, span], ds_sem.at[slot]).start()
            return 0

        def back(u, size):
            o = pl.multiple_of(u * SMALL, SMALL)
            span = pl.ds(o, size)
            w = []
            for i in range(size // PART if size == HUGE else 1):
                part = pl.ds(o + i * PART, PART) if size == HUGE else span
                top = tops[pl.ds(pl.multiple_of((u + i * (PART // SMALL)) * 8, 8), 8), :][:1]
                w.append(exps[part, :] * (jnp.exp2(top - m) * share))
            w = jnp.concatenate(w, axis=0)
            ds = (w * ((gws[span, :] - delta) * SCALE)).astype(bf16)
            ds_out[slot, span, :] = ds
            nt = (((1,), (1,)), ((), ()))
            acc[:, span] += lax.dot_general(qs_t[:KVW], ds, nt, preferred_element_type=f32)
            acc[:LAT, span] += lax.dot_general(dos_t[...], w.astype(bf16), nt, preferred_element_type=f32)
            for k in range(max(size // BIG, 1)):
                leave_ds(u // (BIG // SMALL) + k, 0)
            return 0

        def blank(u, _):
            ds_out[slot, pl.ds(pl.multiple_of(u * SMALL, SMALL), SMALL), :] = jnp.zeros((SMALL, ROWS), bf16)
            return 0

        lax.fori_loop(full + 1, TOKENS // SMALL, blank, 0)
        lax.fori_loop(last // (BIG // SMALL) + 1, QUARTERS, leave_ds, 0)
        lax.fori_loop(0, huge, lambda t, _: back(t * (HUGE // SMALL), HUGE), 0)
        lax.fori_loop(0, big, lambda t, _: back(huge * (HUGE // SMALL), BIG), 0)
        lax.switch(over, [lambda n=n: back(last, n * SMALL) for n in range(1, BIG // SMALL + 1)])

        return 0

    lax.fori_loop(0, CHUNKS, chunk, 0)
    copy_keys.wait()

    def leave(j, _):
        o = pl.multiple_of(j * 256, 256)
        keys[pl.ds(o, 256), :KVW] = acc[:, pl.ds(o, 256)].astype(bf16).T
        for i in range(4):
            pltpu.make_async_copy(keys.at[pl.ds(o + i * RUN, RUN)], part_ref.at[chip_of[j * 4 + i]], out_sem.at[0]).start()
        return 0

    lax.fori_loop(0, TOKENS // 256, leave, 0)
    for slot in range(2):
        pltpu.make_async_copy(ds_out.at[slot], ds_ref.at[0], ds_sem.at[slot]).wait()
    pltpu.make_async_copy(keys, keys, out_sem.at[0]).wait()


def attend(positions, runs, query, out_grad, gathered):
    V, f32, bf16 = pltpu.VMEM, jnp.float32, jnp.bfloat16
    return pl.pallas_call(
        attend_kernel,
        out_shape=(jax.ShapeDtypeStruct((CHUNKS, TOKENS, ROWS), bf16), jax.ShapeDtypeStruct((TOKENS, PAD), bf16),
                   jax.ShapeDtypeStruct((RUNS, RUN, PAD), bf16)),
        in_specs=[pl.BlockSpec(memory_space=pltpu.SMEM)] * 2 + [pl.BlockSpec(memory_space=pltpu.HBM)] * 3,
        out_specs=(pl.BlockSpec(memory_space=pltpu.HBM),) * 3,
        scratch_shapes=[
            pltpu.SMEM((RUNS,), jnp.int32),
            V((TOKENS, PAD), bf16), V((KVW, TOKENS), f32),
            V((TOKENS, ROWS), f32), V((TOKENS, ROWS), f32), V((TOKENS // SMALL * 8, ROWS), f32),
            V((ROWS, PAD), bf16), V((PAD, ROWS), bf16), V((ROWS, LAT), bf16), V((LAT, ROWS), bf16),
            V((2 * RUN, HEADS * KVW), bf16), V((2 * RUN, HEADS * LAT), bf16), V((2, TOKENS, ROWS), bf16),
            pltpu.SemaphoreType.DMA((TOKENS // BIG,)), pltpu.SemaphoreType.DMA((2, CHUNKS)), pltpu.SemaphoreType.DMA((2,)), pltpu.SemaphoreType.DMA((2,)),
        ],
        compiler_params=pltpu.CompilerParams(vmem_limit_bytes=62 * 2**20),
        cost_estimate=pl.CostEstimate(flops=46 * 10**9, bytes_accessed=2 * 10**7, transcendentals=10**7),
        name="attend",
    )(positions, runs, query, out_grad, gathered)


def settle_kernel(qg_in, lg_in, qg_ref, lg_ref, qg_buf, lg_buf, sem):
    pieces = [(qg_in.at[pl.ds(i * 16, 16)], qg_buf.at[pl.ds(i * 16, 16)], qg_ref.at[pl.ds(i * 16, 16)]) for i in range(8)]
    pieces.append((lg_in, lg_buf, lg_ref))
    loads = [pltpu.make_async_copy(a, b, sem.at[0, i]) for i, (a, b, _) in enumerate(pieces)]
    stores = [pltpu.make_async_copy(b, c, sem.at[1, i]) for i, (_, b, c) in enumerate(pieces)]
    for load in loads:
        load.start()
    for load, store in zip(loads, stores):
        load.wait()
        store.start()
    for store in stores:
        store.wait()


def settle(query_grad, latent_grad):
    return pl.pallas_call(
        settle_kernel,
        out_shape=(jax.ShapeDtypeStruct(query_grad.shape, query_grad.dtype), jax.ShapeDtypeStruct(latent_grad.shape, latent_grad.dtype)),
        in_specs=[pl.BlockSpec(memory_space=pltpu.HBM), pl.BlockSpec(memory_space=pl.ANY)],
        out_specs=(pl.BlockSpec(memory_space=pltpu.HBM),) * 2,
        scratch_shapes=[pltpu.VMEM(query_grad.shape, query_grad.dtype), pltpu.VMEM(latent_grad.shape, latent_grad.dtype), pltpu.SemaphoreType.DMA((2, 9))],
        cost_estimate=pl.CostEstimate(flops=0, bytes_accessed=5 * 10**6, transcendentals=0),
        name="settle",
    )(query_grad, latent_grad)


def per_device(query, latent, out_grad, positions):
    gathered, runs = gather(positions, latent)
    ds, keys, part = attend(positions, runs, query, out_grad, gathered.reshape(RUNS, RUN, PAD))
    latent_grad, query_grad = scatter(part.reshape(4, 4, 4, RUN, PAD), ds, keys)
    return settle(query_grad, latent_grad)


def solution(mesh):
    return jax.shard_map(
        per_device,
        mesh=mesh,
        in_specs=(P("seq", "tp"), P(("seq", "tp"), None), P("seq", "tp"), P("seq")),
        out_specs=(P("seq", "tp"), P(("seq", "tp"), None)),
        check_vma=False,
    )
```
